512 devices in a mesh: section: 32 (over y_hi, z), dp: 16 (over y_lo, x, core).
Axes of the slice: x: 4, y: 4 (y_hi: 2, y_lo: 2; y = y_hi * 2 + y_lo), z: 16, core: 2. Of those that a mesh axis runs over, the one named last changes fastest.
Arguments:
- section_inputs: bfloat16 [2, 32, 512, 8192], P(None, 'section', 'dp'), may hold values from -6 to 6
- out_grads: bfloat16 [2, 32, 512, 8192], P(None, 'section', 'dp'), may hold values from -6 to 6
- adapters: bfloat16 [2, 32, 2, 64, 8192], P(None, 'section', None, None, 'dp'), as said below
Outputs:
- next_inputs: bfloat16 [2, 32, 512, 8192], P(None, 'section', 'dp')
- prev_grads: bfloat16 [2, 32, 512, 8192], P(None, 'section', 'dp')
- adapter_grads: float32 [2, 32, 2, 64, 8192], P(None, 'section', None, None, 'dp')
The draws below stay inside these ranges and needn't reach their ends.
Inputs may be any that keep to these rules, and one draw needn't show every extreme that they name: adapters[1, p] equals adapters[0, 31 - p] for every p.
All inputs are finite; a program needn't handle non-finite values.
Results may differ from the reference program's by a relative error of at most 0.02.
Values may be sent and summed in bfloat16 or wider, within the bound.
No kernel may reach another device: no remote copies, remote signals or barrier semaphores. Data moves between devices by JAX's collectives and lax.ppermute only.
A program may use at most 64 MiB of HBM per device.

```python
import jax
import jax.numpy as jnp
from jax import lax

D = 8192
RANK = 64
TOK = 32
SECTIONS = 32
TOKENS = 512
N_DP = 16


def draw_adapters(key, part):
    key = jax.random.fold_in(key, 7)
    base = jax.random.normal(key, (SECTIONS, 2, RANK, D), jnp.float32)
    factor = jnp.array([D ** (-0.5), RANK ** (-0.5)], jnp.float32).reshape(1, 2, 1, 1)
    base = base * factor
    return jnp.stack([base, base[::-1]]).astype(jnp.bfloat16)


def levels(stream_key, shape, cuts, smallest, top_value):
    def one(dim, shards_of):
        steps = jax.random.uniform(jax.random.fold_in(jax.random.fold_in(stream_key, 6), dim), (shards_of,), jnp.float32, smallest / len(cuts), top_value / len(cuts))
        return jnp.repeat(jnp.exp(steps), shape[dim] // shards_of).reshape((-1,) + (1,) * (len(shape) - dim - 1))

    level = one(*cuts[0])
    for cut in cuts[1:]:
        level = level * one(*cut)
    return level


def noise(key, extent, width, bound, cuts=(), dtype=jnp.bfloat16):
    values = width * jax.random.normal(key, extent, jnp.float32)
    if cuts:
        values = values * levels(key, extent, cuts, -0.22, 0.18)
    return jnp.clip(values, -bound, bound).astype(dtype)


def setup_inputs(seed: int = 0) -> dict:
    key_of = jax.random.split(jax.random.key(seed), 4)
    section_inputs = noise(key_of[0], (2, SECTIONS, TOKENS, D), 1.0, 6.0, ((1, 32), (2, 16)))
    out_grads = noise(key_of[1], (2, SECTIONS, TOKENS, D), 1.0, 6.0, ((1, 32), (2, 16)))
    adapters = draw_adapters(jax.random.fold_in(key_of[3], 71), 0)
    return {"section_inputs": section_inputs, "out_grads": out_grads, "adapters": adapters}


def section_pass(inputs, grads, down_map, up_map):
    xf = inputs.astype(jnp.float32)
    scale = lax.rsqrt(lax.optimization_barrier(jnp.mean(xf * xf, axis=-1, keepdims=True)) + 1e-05)
    normed = (xf * scale).astype(jnp.bfloat16)
    pre = jnp.dot(normed, down_map.T, preferred_element_type=jnp.float32)
    sig = jax.nn.sigmoid(pre)
    hidden = (pre * sig).astype(jnp.bfloat16)
    output = (xf + jnp.dot(hidden, up_map, preferred_element_type=jnp.float32)).astype(jnp.bfloat16)
    dhidden = jnp.dot(grads, up_map.T, preferred_element_type=jnp.float32)
    dpre = (dhidden * (sig * (1.0 + pre * (1.0 - sig)))).astype(jnp.bfloat16)
    dnorm = jnp.dot(dpre, down_map, preferred_element_type=jnp.float32)
    inner = lax.optimization_barrier(jnp.mean(dnorm * xf, axis=-1, keepdims=True))
    dinput = (grads.astype(jnp.float32) + scale * (dnorm - xf * inner * scale * scale)).astype(jnp.bfloat16)
    part_a = jnp.dot(dpre.T, normed, preferred_element_type=jnp.float32).astype(jnp.bfloat16)
    part_b = jnp.dot(hidden.T, grads, preferred_element_type=jnp.float32).astype(jnp.bfloat16)
    return (output, dinput, jnp.stack([part_a, part_b]))

def held_section(inputs, grads, weights):
    rows_in = inputs.reshape(N_DP, TOK, D)
    rows_grad = grads.reshape(N_DP, TOK, D)
    output, dinput, parts = jax.vmap(lambda a, b: section_pass(a, b, weights[0], weights[1]))(rows_in, rows_grad)
    return (output.reshape(TOKENS, D), dinput.reshape(TOKENS, D), lax.optimization_barrier(jnp.sum(parts.astype(jnp.float32), axis=0)))

def position(items):
    inputs, grads, weights = items
    down = held_section(inputs[0], grads[0], weights[0])
    upper = held_section(inputs[1], grads[1], weights[1])
    return (jnp.stack([down[0], upper[0]]), jnp.stack([down[1], upper[1]]), jnp.stack([down[2], upper[2]]))

def reference(section_inputs, out_grads, adapters):
    outputs, dinputs, sums = lax.map(position, (jnp.swapaxes(section_inputs, 0, 1), jnp.swapaxes(out_grads, 0, 1), jnp.swapaxes(adapters, 0, 1)))
    blank = jnp.zeros((1, TOKENS, D), jnp.bfloat16)
    next_down = jnp.concatenate([blank, outputs[:-1, 0]], axis=0)
    next_up = jnp.concatenate([outputs[1:, 1], blank], axis=0)
    prev_down = jnp.concatenate([dinputs[1:, 0], blank], axis=0)
    prev_up = jnp.concatenate([blank, dinputs[:-1, 1]], axis=0)
    flipped = sums[::-1]
    grads_down = sums[:, 0] + flipped[:, 1]
    grads_up = sums[:, 1] + flipped[:, 0]
    return (jnp.stack([next_down, next_up]), jnp.stack([prev_down, prev_up]), jnp.stack([grads_down, grads_up]))
```

```python
import jax
import jax.numpy as jnp
from jax import lax
from jax.sharding import PartitionSpec as P


def passed_along(value, axis, steps):
    count = lax.axis_size(axis)
    first, last = (max(0, -steps), min(count, count - steps))
    return lax.ppermute(value, axis, [(source, source + steps) for source in range(first, last)])


def section_pass(inputs, grads, down_map, up_map):
    xf = inputs.astype(jnp.float32)
    scale = lax.rsqrt(jnp.mean(xf * xf, axis=-1, keepdims=True) + 1e-05)
    normed = (xf * scale).astype(jnp.bfloat16)
    pre = jnp.dot(normed, down_map.T, preferred_element_type=jnp.float32)
    sig = jax.nn.sigmoid(pre)
    hidden = (pre * sig).astype(jnp.bfloat16)
    output = (xf + jnp.dot(hidden, up_map, preferred_element_type=jnp.float32)).astype(jnp.bfloat16)
    dhidden = jnp.dot(grads, up_map.T, preferred_element_type=jnp.float32)
    dpre = (dhidden * (sig * (1.0 + pre * (1.0 - sig)))).astype(jnp.bfloat16)
    dnorm = jnp.dot(dpre, down_map, preferred_element_type=jnp.float32)
    inner = jnp.mean(dnorm * xf, axis=-1, keepdims=True)
    dinput = (grads.astype(jnp.float32) + scale * (dnorm - xf * inner * scale * scale)).astype(
        jnp.bfloat16
    )
    part_a = jnp.dot(dpre.T, normed, preferred_element_type=jnp.float32).astype(jnp.bfloat16)
    part_b = jnp.dot(hidden.T, grads, preferred_element_type=jnp.float32).astype(jnp.bfloat16)
    return (output, dinput, jnp.stack([part_a, part_b]))


def shards(section_inputs, out_grads, adapters):
    weights = lax.all_gather(adapters, "dp", axis=4, tiled=True)
    down_out, down_din, down_parts = section_pass(
        section_inputs[0, 0], out_grads[0, 0], weights[0, 0, 0], weights[0, 0, 1]
    )
    up_out, up_din, up_parts = section_pass(
        section_inputs[1, 0], out_grads[1, 0], weights[1, 0, 0], weights[1, 0, 1]
    )
    from_lower = passed_along((down_out, up_din), "section", 1)
    from_upper = passed_along((up_out, down_din), "section", -1)
    next_inputs = jnp.stack([from_lower[0], from_upper[0]])[:, None]
    prev_grads = jnp.stack([from_upper[1], from_lower[1]])[:, None]
    partials = jnp.stack([down_parts, up_parts])
    shares = lax.psum_scatter(partials, "dp", scatter_dimension=3, tiled=True)
    count = lax.axis_size("section")
    partner = lax.ppermute(shares, "section", [(i, count - 1 - i) for i in range(count)])
    shares = shares.astype(jnp.float32)
    partner = partner.astype(jnp.float32)
    summed = jnp.stack([shares[0] + partner[1], shares[1] + partner[0]])
    return (next_inputs, prev_grads, summed[:, None])


def solution(mesh):
    in_specs = (
        P(None, "section", "dp", None),
        P(None, "section", "dp", None),
        P(None, "section", None, None, "dp"),
    )
    out_specs = (
        P(None, "section", "dp", None),
        P(None, "section", "dp", None),
        P(None, "section", None, None, "dp"),
    )
    return jax.shard_map(shards, mesh=mesh, in_specs=in_specs, out_specs=out_specs, check_vma=False)
```

```python
import jax
import jax.numpy as jnp
from jax import lax
from jax.experimental import pallas as pl
from jax.experimental.pallas import tpu as pltpu
from jax.sharding import PartitionSpec as P


def adapter_kernel(core_ref, x_ref, g_ref, taken_ref, w_ref, up_ref, down_ref, part_ref):
    core = core_ref[0]
    is_down = core == 0
    slices, _, rank, width = w_ref.shape
    tokens, model = 2 * x_ref.shape[1], x_ref.shape[2]
    across = (((1,), (1,)), ((), ()))
    over_tokens = (((0,), (0,)), ((), ()))
    f32 = jnp.float32

    def columns(i):
        cols = pl.ds(i * width, width)
        x = jnp.concatenate([x_ref[core, :, cols], taken_ref[0, :, cols]], axis=0)
        g = jnp.concatenate([g_ref[core, :, cols], taken_ref[1, :, cols]], axis=0)
        return cols, x, g

    u = jnp.zeros((tokens, rank), f32)
    v = jnp.zeros((tokens, rank), f32)
    squares = jnp.zeros((tokens, 128), f32)
    for i in range(slices):
        _, x, g = columns(i)
        u += lax.dot_general(x, w_ref[i, 0], across, preferred_element_type=f32)
        v += lax.dot_general(g, w_ref[i, 1], across, preferred_element_type=f32)
        xf = x.astype(f32)
        for j in range(width // 128):
            piece = xf[:, j * 128:(j + 1) * 128]
            squares += piece * piece
    scale = lax.rsqrt(jnp.sum(squares, axis=1, keepdims=True) / model + 1e-05)
    pre = scale * u
    sig = jax.nn.sigmoid(pre)
    hidden = (pre * sig).astype(jnp.bfloat16)
    dpre = v * (sig * (1.0 + pre * (1.0 - sig)))
    inner = jnp.sum(dpre * u, axis=1, keepdims=True) / model
    scaled = (scale * dpre).astype(jnp.bfloat16)
    back = inner * scale * scale * scale
    for i in range(slices):
        cols, x, g = columns(i)
        xf, gf = x.astype(f32), g.astype(f32)
        part_ref[i, 0] = lax.dot_general(scaled, x, over_tokens, preferred_element_type=f32).astype(part_ref.dtype)
        part_ref[i, 1] = lax.dot_general(hidden, g, over_tokens, preferred_element_type=f32).astype(part_ref.dtype)
        y = xf + jnp.dot(hidden, w_ref[i, 1], preferred_element_type=f32)
        dx = gf + jnp.dot(scaled, w_ref[i, 0], preferred_element_type=f32) - xf * back
        up_ref[:, cols] = jnp.where(is_down, y, dx).astype(up_ref.dtype)
        down_ref[:, cols] = jnp.where(is_down, dx, y).astype(down_ref.dtype)


def adapter(core, x, g, taken, w):
    tokens, model = 2 * x.shape[1], x.shape[2]
    whole = pl.BlockSpec(memory_space=pltpu.VMEM)
    relayed = jax.ShapeDtypeStruct((tokens, model), x.dtype)
    return pl.pallas_call(
        adapter_kernel,
        out_shape=(relayed, relayed, jax.ShapeDtypeStruct(w.shape, w.dtype)),
        in_specs=[pl.BlockSpec(memory_space=pltpu.SMEM)] + [whole] * 4,
        out_specs=(whole,) * 3,
        compiler_params=pltpu.CompilerParams(vmem_limit_bytes=8 << 20),
        cost_estimate=pl.CostEstimate(flops=6 * tokens * w.size, bytes_accessed=16 << 20, transcendentals=0),
    )(jnp.full((1,), core, jnp.int32), x, g, taken, w)


def shards(section_inputs, out_grads, adapters):
    n_dp = lax.axis_size("dp")
    count = lax.axis_size("section")
    half = count // 2
    section = lax.axis_index("section")
    core = lax.axis_index("dp") % 2
    is_down = core == 0
    tokens = section_inputs.shape[2]
    swap = [(i, i ^ 1) for i in range(n_dp)]
    weights = adapters[:, 0]
    inputs, grads = section_inputs[:, 0], out_grads[:, 0]

    to_all = jnp.broadcast_to(weights[None], (n_dp // 2,) + weights.shape).reshape((n_dp,) + weights.shape[1:])
    gathered = lax.all_to_all(to_all, "dp", 0, 0, tiled=True)
    given = jnp.stack([jnp.where(is_down, inputs[1], inputs[0]), jnp.where(is_down, grads[1], grads[0])])
    taken = lax.ppermute(given, "dp", swap)
    up, down, parts = adapter(core, inputs, grads, taken, gathered)

    terms = lax.all_to_all(parts, "dp", 0, 0, tiled=True)
    sums = jnp.sum(terms.reshape((n_dp // 2, 2) + terms.shape[1:]).astype(jnp.float32), axis=0)

    up = lax.ppermute(up, "section", [(i, i + 1) for i in range(count - 1) if i != half - 1] + [(half - 1, 0)])
    down = lax.ppermute(down, "section", [(i, i - 1) for i in range(1, count) if i != half] + [(half, count - 1)])
    other = lax.ppermute(jnp.stack([up[tokens:], down[tokens:]]), "dp", swap)
    up = jnp.stack([up[:tokens], other[0]])
    down = jnp.stack([down[:tokens], other[1]])
    crossing = lax.ppermute(jnp.where(section == 0, up, down), "section", [(0, half), (count - 1, half - 1)])
    none = jnp.zeros_like(up)
    up = jnp.where(section == half, crossing, jnp.where(section == 0, none, up))
    down = jnp.where(section == half - 1, crossing, jnp.where(section == count - 1, none, down))
    next_inputs = jnp.where(is_down, jnp.stack([up[0], down[1]]), jnp.stack([up[1], down[0]]))
    prev_grads = jnp.where(is_down, jnp.stack([down[0], up[1]]), jnp.stack([down[1], up[0]]))

    partner = lax.ppermute(sums.astype(jnp.bfloat16), "section", [(i, count - 1 - i) for i in range(count)])
    summed = sums + partner[::-1].astype(jnp.float32)
    return (next_inputs[:, None], prev_grads[:, None], summed[:, None])


def solution(mesh):
    in_specs = (
        P(None, "section", "dp", None),
        P(None, "section", "dp", None),
        P(None, "section", None, None, "dp"),
    )
    out_specs = (
        P(None, "section", "dp", None),
        P(None, "section", "dp", None),
        P(None, "section", None, None, "dp"),
    )
    return jax.shard_map(shards, mesh=mesh, in_specs=in_specs, out_specs=out_specs, check_vma=False)
```

```python
import jax
import jax.numpy as jnp
from jax import lax
from jax.experimental import pallas as pl
from jax.experimental.pallas import tpu as pltpu
from jax.sharding import PartitionSpec as P

WHOLE = pl.BlockSpec(memory_space=pltpu.VMEM)
ANYWHERE = pl.BlockSpec(memory_space=pl.ANY)
SCALARS = pl.BlockSpec(memory_space=pltpu.SMEM)
ACROSS = (((1,), (1,)), ((), ()))
OVER_TOKENS = (((0,), (0,)), ((), ()))
PARAMS = pltpu.CompilerParams(vmem_limit_bytes=12 << 20)
F32 = jnp.float32


def spread_kernel(w_ref, out_ref, sems):
    copies = [
        pltpu.make_async_copy(w_ref, out_ref.at[pl.ds(2 * i, 2)], sems.at[i]) for i in range(out_ref.shape[0] // 2)
    ]
    for copy in copies:
        copy.start()
    for copy in copies:
        copy.wait()


def spread(w, n_dp):
    return pl.pallas_call(
        spread_kernel,
        out_shape=pltpu.HBM((n_dp,) + w.shape[1:], w.dtype),
        in_specs=[WHOLE],
        out_specs=ANYWHERE,
        scratch_shapes=[pltpu.SemaphoreType.DMA((n_dp // 2,))],
        compiler_params=PARAMS,
        cost_estimate=pl.CostEstimate(flops=0, bytes_accessed=n_dp * w.size, transcendentals=0),
    )(w)


def adapter_kernel(
    core_ref, x_ref, g_ref, taken_ref, w_ref, up_ref, down_ref, send_ref, part_ref, xs, gs, ps, ms, loads, part_stores, stores
):
    core = core_ref[0]
    is_down = core == 0
    slices, _, rank, width = w_ref.shape
    tokens, model = x_ref.shape[1:]
    chunks = loads.shape[0]
    own, others = pl.ds(0, tokens), pl.ds(tokens, tokens)

    fetches = []
    for j in range(chunks):
        cols = pl.ds(j * (model // chunks), model // chunks)
        fetches.append([
            pltpu.make_async_copy(x_ref.at[core, :, cols], xs.at[own, cols], loads.at[j, 0]),
            pltpu.make_async_copy(taken_ref.at[0, :, cols], xs.at[others, cols], loads.at[j, 1]),
            pltpu.make_async_copy(g_ref.at[core, :, cols], gs.at[own, cols], loads.at[j, 2]),
            pltpu.make_async_copy(taken_ref.at[1, :, cols], gs.at[others, cols], loads.at[j, 3]),
        ])
        for copy in fetches[-1]:
            copy.start()

    u = jnp.zeros((2 * tokens, rank), F32)
    v = jnp.zeros((2 * tokens, rank), F32)
    squares = jnp.zeros((2 * tokens, 128), F32)
    for i in range(slices):
        if i % (slices // chunks) == 0:
            for copy in fetches[i // (slices // chunks)]:
                copy.wait()
        cols = pl.ds(i * width, width)
        x = xs[:, cols]
        u += lax.dot_general(x, w_ref[i, 0], ACROSS, preferred_element_type=F32)
        v += lax.dot_general(gs[:, cols], w_ref[i, 1], ACROSS, preferred_element_type=F32)
        xf = x.astype(F32)
        for j in range(width // 128):
            piece = xf[:, j * 128:(j + 1) * 128]
            squares += piece * piece
    scale = lax.rsqrt(jnp.sum(squares, axis=1, keepdims=True) / model + 1e-05)
    pre = scale * u
    sig = jax.nn.sigmoid(pre)
    hidden = (pre * sig).astype(jnp.bfloat16)
    dpre = v * (sig * (1.0 + pre * (1.0 - sig)))
    inner = jnp.sum(dpre * u, axis=1, keepdims=True) / model
    scaled = (scale * dpre).astype(jnp.bfloat16)
    back = inner * scale * scale * scale

    stored = []
    per = slices // chunks
    for i in range(slices):
        cols = pl.ds(i * width, width)
        ps[i, 0] = lax.dot_general(scaled, xs[:, cols], OVER_TOKENS, preferred_element_type=F32).astype(ps.dtype)
        ps[i, 1] = lax.dot_general(hidden, gs[:, cols], OVER_TOKENS, preferred_element_type=F32).astype(ps.dtype)
        if i % per == per - 1:
            some = pl.ds(i + 1 - per, per)
            stored.append(pltpu.make_async_copy(ps.at[some], part_ref.at[some], part_stores.at[i // per]))
            stored[-1].start()
    for i in range(slices):
        cols = pl.ds(i * width, width)
        xf, gf = xs[:, cols].astype(F32), gs[:, cols].astype(F32)
        y = (xf + jnp.dot(hidden, w_ref[i, 1], preferred_element_type=F32)).astype(ms.dtype)
        dx = (gf + jnp.dot(scaled, w_ref[i, 0], preferred_element_type=F32) - xf * back).astype(ms.dtype)
        ms[0, :, cols] = jnp.where(is_down, y, dx)
        ms[1, :, cols] = jnp.where(is_down, dx, y)
        if i % per == per - 1:
            j = i // per
            cols = pl.ds(j * (model // chunks), model // chunks)
            for copy in (
                pltpu.make_async_copy(ms.at[0, own, cols], up_ref.at[:, cols], stores.at[j, 0]),
                pltpu.make_async_copy(ms.at[1, own, cols], down_ref.at[:, cols], stores.at[j, 1]),
                pltpu.make_async_copy(ms.at[0, others, cols], send_ref.at[0, :, cols], stores.at[j, 2]),
                pltpu.make_async_copy(ms.at[1, others, cols], send_ref.at[1, :, cols], stores.at[j, 3]),
            ):
                copy.start()
                stored.append(copy)
    for copy in stored:
        copy.wait()


def adapter(core, x, g, taken, w):
    tokens, model = x.shape[1:]
    one = pltpu.HBM((tokens, model), x.dtype)
    both = pltpu.VMEM((2 * tokens, model), x.dtype)
    return pl.pallas_call(
        adapter_kernel,
        out_shape=(one, one, pltpu.HBM((2, tokens, model), x.dtype), pltpu.HBM(w.shape, w.dtype)),
        in_specs=[SCALARS] + [ANYWHERE] * 3 + [WHOLE],
        out_specs=(ANYWHERE,) * 4,
        scratch_shapes=[
            both,
            both,
            pltpu.VMEM(w.shape, w.dtype),
            pltpu.VMEM((2, 2 * tokens, model), x.dtype),
            pltpu.SemaphoreType.DMA((4, 4)),
            pltpu.SemaphoreType.DMA((4,)),
            pltpu.SemaphoreType.DMA((4, 4)),
        ],
        compiler_params=PARAMS,
        cost_estimate=pl.CostEstimate(flops=12 * tokens * w.size, bytes_accessed=12 << 20, transcendentals=0),
    )(core, *(pltpu.with_memory_space_constraint(a, pltpu.HBM) for a in (x, g, taken)), w)


def add_kernel(sums_ref, partner_ref, out_ref):
    out_ref[0] = sums_ref[0] + partner_ref[1].astype(F32)
    out_ref[1] = sums_ref[1] + partner_ref[0].astype(F32)


def add_mirrored(sums, partner):
    return pl.pallas_call(
        add_kernel,
        out_shape=jax.ShapeDtypeStruct(sums.shape, F32),
        in_specs=[WHOLE] * 2,
        out_specs=WHOLE,
        compiler_params=PARAMS,
        cost_estimate=pl.CostEstimate(flops=0, bytes_accessed=2 << 20, transcendentals=0),
    )(sums, partner)


def moved(value, pairs, n_dp, flip=()):
    turn = n_dp // 2
    routes = [(a * n_dp + d, b * n_dp + d) for a, b in pairs for d in range(n_dp)]
    routes += [(a * n_dp + d, b * n_dp + (d ^ turn)) for a, b in flip for d in range(n_dp)]
    return lax.ppermute(value, ("section", "dp"), routes)


def shards(section_inputs, out_grads, adapters):
    n_dp = lax.axis_size("dp")
    count = lax.axis_size("section")
    half = count // 2
    section = lax.axis_index("section")
    core = lax.axis_index("dp") % 2
    is_down = core == 0
    swap = [(i, i ^ 1) for i in range(n_dp)]
    which = jnp.full((1,), core, jnp.int32)
    inputs, grads = section_inputs[:, 0], out_grads[:, 0]

    gathered = lax.all_to_all(spread(adapters[:, 0], n_dp), "dp", 0, 0, tiled=True)
    given = jnp.stack([jnp.where(is_down, inputs[1], inputs[0]), jnp.where(is_down, grads[1], grads[0])])
    taken = lax.ppermute(given, "dp", swap)
    up_own, down_own, send, parts = adapter(which, inputs, grads, taken, gathered)

    terms = lax.all_to_all(parts, "dp", 0, 0, tiled=True)
    sums = jnp.sum(terms.reshape((n_dp // 2, 2) + terms.shape[1:]).astype(F32), axis=0)

    got = lax.ppermute(send, "dp", swap)
    up_own, down_own, up_got, down_got = lax.optimization_barrier((up_own, down_own, got[0], got[1]))
    ups = [(i, i + 1) for i in range(count - 1) if i != half - 1]
    downs = [(i, i - 1) for i in range(1, count) if i != half]
    up_own = moved(up_own, ups, n_dp, [(half - 1, half)])
    down_own = moved(down_own, downs, n_dp, [(half, half - 1)])
    up_got = moved(up_got, ups + [(half - 1, 0)], n_dp)
    down_got = moved(down_got, downs + [(half, count - 1)], n_dp)
    sums, up_own, down_own, up_got, down_got = lax.optimization_barrier((sums, up_own, down_own, up_got, down_got))

    partner = lax.ppermute(sums.astype(jnp.bfloat16), "section", [(i, count - 1 - i) for i in range(count)])
    crossed_own = moved(
        jnp.where(section == half, up_own, down_own), [], n_dp, [(half, half), (half - 1, half - 1)]
    )
    crossed_got = moved(jnp.where(section == 0, up_got, down_got), [(0, half), (count - 1, half - 1)], n_dp)
    none = jnp.zeros_like(up_got)
    up_own = jnp.where(section == half, crossed_own, up_own)
    down_own = jnp.where(section == half - 1, crossed_own, down_own)
    up_got = jnp.where(section == half, crossed_got, jnp.where(section == 0, none, up_got))
    down_got = jnp.where(section == half - 1, crossed_got, jnp.where(section == count - 1, none, down_got))
    next_inputs = jnp.stack([jnp.where(is_down, up_own, up_got), jnp.where(is_down, down_got, down_own)])
    prev_grads = jnp.stack([jnp.where(is_down, down_own, down_got), jnp.where(is_down, up_got, up_own)])

    summed = add_mirrored(sums, partner)
    return (next_inputs[:, None], prev_grads[:, None], summed[:, None])


def solution(mesh):
    in_specs = (
        P(None, "section", "dp", None),
        P(None, "section", "dp", None),
        P(None, "section", None, None, "dp"),
    )
    out_specs = (
        P(None, "section", "dp", None),
        P(None, "section", "dp", None),
        P(None, "section", None, None, "dp"),
    )
    return jax.shard_map(shards, mesh=mesh, in_specs=in_specs, out_specs=out_specs, check_vma=False)
```

```python
import functools

import jax
import jax.numpy as jnp
from jax import lax
from jax.experimental import pallas as pl
from jax.experimental.pallas import tpu as pltpu
from jax.sharding import PartitionSpec as P

WHOLE = pl.BlockSpec(memory_space=pltpu.VMEM)
ANYWHERE = pl.BlockSpec(memory_space=pl.ANY)
SCALARS = pl.BlockSpec(memory_space=pltpu.SMEM)
ACROSS = (((1,), (1,)), ((), ()))
OVER_TOKENS = (((0,), (0,)), ((), ()))
PARAMS = pltpu.CompilerParams(vmem_limit_bytes=12 << 20)
F32 = jnp.float32


def spread_kernel(w_ref, out_ref, sems):
    copies = [
        pltpu.make_async_copy(w_ref, out_ref.at[pl.ds(2 * i, 2)], sems.at[i]) for i in range(out_ref.shape[0] // 2)
    ]
    for copy in copies:
        copy.start()
    for copy in copies:
        copy.wait()


def spread(w, n_dp):
    return pl.pallas_call(
        spread_kernel,
        out_shape=pltpu.HBM((n_dp,) + w.shape[1:], w.dtype),
        in_specs=[WHOLE],
        out_specs=ANYWHERE,
        scratch_shapes=[pltpu.SemaphoreType.DMA((n_dp // 2,))],
        compiler_params=PARAMS,
        cost_estimate=pl.CostEstimate(flops=0, bytes_accessed=n_dp * w.size, transcendentals=0),
    )(w)


def fetch(core, x_ref, g_ref, taken_ref, xs, gs, sems):
    tokens, model = x_ref.shape[1:]
    chunks = sems.shape[0]
    own, others = pl.ds(0, tokens), pl.ds(tokens, tokens)
    copies = []
    for j in range(chunks):
        cols = pl.ds(j * (model // chunks), model // chunks)
        copies.append([
            pltpu.make_async_copy(x_ref.at[core, :, cols], xs.at[own, cols], sems.at[j, 0]),
            pltpu.make_async_copy(taken_ref.at[0, :, cols], xs.at[others, cols], sems.at[j, 1]),
            pltpu.make_async_copy(g_ref.at[core, :, cols], gs.at[own, cols], sems.at[j, 2]),
            pltpu.make_async_copy(taken_ref.at[1, :, cols], gs.at[others, cols], sems.at[j, 3]),
        ])
        for copy in copies[-1]:
            copy.start()
    return copies


def partials_kernel(
    core_ref, x_ref, g_ref, taken_ref, w_ref, part_ref, hidden_ref, scaled_ref, back_ref, xs, gs, ps, loads, stores
):
    slices, _, rank, width = w_ref.shape
    tokens, model = xs.shape
    chunks = loads.shape[0]
    per = slices // chunks
    fetches = fetch(core_ref[0], x_ref, g_ref, taken_ref, xs, gs, loads)

    u = jnp.zeros((tokens, rank), F32)
    v = jnp.zeros((tokens, rank), F32)
    squares = jnp.zeros((tokens, 128), F32)
    for i in range(slices):
        if i % per == 0:
            for copy in fetches[i // per]:
                copy.wait()
        cols = pl.ds(i * width, width)
        x = xs[:, cols]
        u += lax.dot_general(x, w_ref[i, 0], ACROSS, preferred_element_type=F32)
        v += lax.dot_general(gs[:, cols], w_ref[i, 1], ACROSS, preferred_element_type=F32)
        xf = x.astype(F32)
        for j in range(width // 128):
            piece = xf[:, j * 128:(j + 1) * 128]
            squares += piece * piece
    scale = lax.rsqrt(jnp.sum(squares, axis=1, keepdims=True) / model + 1e-05)
    pre = scale * u
    sig = jax.nn.sigmoid(pre)
    hidden = (pre * sig).astype(jnp.bfloat16)
    dpre = v * (sig * (1.0 + pre * (1.0 - sig)))
    inner = jnp.sum(dpre * u, axis=1, keepdims=True) / model
    scaled = (scale * dpre).astype(jnp.bfloat16)
    hidden_ref[...] = hidden
    scaled_ref[...] = scaled
    back_ref[...] = jnp.broadcast_to(inner * scale * scale * scale, back_ref.shape)

    stored = []
    for i in range(slices):
        cols = pl.ds(i * width, width)
        ps[i, 0] = lax.dot_general(scaled, xs[:, cols], OVER_TOKENS, preferred_element_type=F32).astype(ps.dtype)
        ps[i, 1] = lax.dot_general(hidden, gs[:, cols], OVER_TOKENS, preferred_element_type=F32).astype(ps.dtype)
        if i % per == per - 1:
            some = pl.ds(i + 1 - per, per)
            stored.append(pltpu.make_async_copy(ps.at[some], part_ref.at[some], stores.at[i // per]))
            stored[-1].start()
    for copy in stored:
        copy.wait()


def partials(core, x, g, taken, w):
    tokens, model, rank = 2 * x.shape[1], x.shape[2], w.shape[2]
    both = pltpu.VMEM((tokens, model), x.dtype)
    inside = jax.ShapeDtypeStruct((tokens, rank), x.dtype)
    return pl.pallas_call(
        partials_kernel,
        out_shape=(pltpu.HBM(w.shape, w.dtype), inside, inside, jax.ShapeDtypeStruct((tokens, 128), F32)),
        in_specs=[SCALARS] + [ANYWHERE] * 3 + [WHOLE],
        out_specs=(ANYWHERE,) + (WHOLE,) * 3,
        scratch_shapes=[
            both,
            both,
            pltpu.VMEM(w.shape, w.dtype),
            pltpu.SemaphoreType.DMA((4, 4)),
            pltpu.SemaphoreType.DMA((4,)),
        ],
        compiler_params=PARAMS,
        cost_estimate=pl.CostEstimate(flops=4 * tokens * w.size, bytes_accessed=8 << 20, transcendentals=0),
    )(core, x, g, taken, w)


def outputs_kernel(
    core_ref, x_ref, g_ref, taken_ref, w_ref, hidden_ref, scaled_ref, back_ref, up_ref, down_ref, send_ref, xs, gs, ms,
    loads, stores
):
    core = core_ref[0]
    is_down = core == 0
    slices, _, rank, width = w_ref.shape
    tokens, model = x_ref.shape[1:]
    chunks = loads.shape[0]
    per = slices // chunks
    own, others = pl.ds(0, tokens), pl.ds(tokens, tokens)
    fetches = fetch(core, x_ref, g_ref, taken_ref, xs, gs, loads)
    hidden, scaled, back = hidden_ref[...], scaled_ref[...], back_ref[:, :1]
    stored = []
    for i in range(slices):
        if i % per == 0:
            for copy in fetches[i // per]:
                copy.wait()
        cols = pl.ds(i * width, width)
        xf, gf = xs[:, cols].astype(F32), gs[:, cols].astype(F32)
        y = (xf + jnp.dot(hidden, w_ref[i, 1], preferred_element_type=F32)).astype(ms.dtype)
        dx = (gf + jnp.dot(scaled, w_ref[i, 0], preferred_element_type=F32) - xf * back).astype(ms.dtype)
        ms[0, :, cols] = jnp.where(is_down, y, dx)
        ms[1, :, cols] = jnp.where(is_down, dx, y)
        if i % per == per - 1:
            j = i // per
            cols = pl.ds(j * (model // chunks), model // chunks)
            for copy in (
                pltpu.make_async_copy(ms.at[0, own, cols], up_ref.at[:, cols], stores.at[j, 0]),
                pltpu.make_async_copy(ms.at[1, own, cols], down_ref.at[:, cols], stores.at[j, 1]),
                pltpu.make_async_copy(ms.at[0, others, cols], send_ref.at[0, :, cols], stores.at[j, 2]),
                pltpu.make_async_copy(ms.at[1, others, cols], send_ref.at[1, :, cols], stores.at[j, 3]),
            ):
                copy.start()
                stored.append(copy)
    for copy in stored:
        copy.wait()


def outputs(core, x, g, taken, w, hidden, scaled, back):
    tokens, model = x.shape[1:]
    one = pltpu.HBM((tokens, model), x.dtype)
    both = pltpu.VMEM((2 * tokens, model), x.dtype)
    return pl.pallas_call(
        outputs_kernel,
        out_shape=(one, one, pltpu.HBM((2, tokens, model), x.dtype)),
        in_specs=[SCALARS] + [ANYWHERE] * 3 + [WHOLE] * 4,
        out_specs=(ANYWHERE,) * 3,
        scratch_shapes=[
            both,
            both,
            pltpu.VMEM((2, 2 * tokens, model), x.dtype),
            pltpu.SemaphoreType.DMA((4, 4)),
            pltpu.SemaphoreType.DMA((4, 4)),
        ],
        compiler_params=PARAMS,
        cost_estimate=pl.CostEstimate(flops=4 * tokens * w.size, bytes_accessed=8 << 20, transcendentals=0),
    )(core, x, g, taken, w, hidden, scaled, back)


def split_kernel(both_ref, first_ref, second_ref, sems):
    copies = [
        pltpu.make_async_copy(both_ref.at[0], first_ref, sems.at[0]),
        pltpu.make_async_copy(both_ref.at[1], second_ref, sems.at[1]),
    ]
    for copy in copies:
        copy.start()
    for copy in copies:
        copy.wait()


def split(both):
    one = pltpu.HBM(both.shape[1:], both.dtype)
    return pl.pallas_call(
        split_kernel,
        out_shape=(one, one),
        in_specs=[ANYWHERE],
        out_specs=(ANYWHERE,) * 2,
        scratch_shapes=[pltpu.SemaphoreType.DMA((2,))],
        compiler_params=PARAMS,
        cost_estimate=pl.CostEstimate(flops=0, bytes_accessed=4 * both.size, transcendentals=0),
    )(both)


def crossing_kernel(count, at_ref, up_own, down_own, up_got, down_got, own_out, got_out, sems):
    section = at_ref[0]
    half = count // 2

    def copy(src, dst, i):
        moving = pltpu.make_async_copy(src, dst, sems.at[i])
        moving.start()
        moving.wait()

    @pl.when(section == half)
    def _():
        copy(up_own, own_out, 0)

    @pl.when(section == half - 1)
    def _():
        copy(down_own, own_out, 0)

    @pl.when(section == 0)
    def _():
        copy(up_got, got_out, 1)

    @pl.when(section == count - 1)
    def _():
        copy(down_got, got_out, 1)


def crossing(count, section, *moved_parts):
    one = pltpu.HBM(moved_parts[0].shape, moved_parts[0].dtype)
    return pl.pallas_call(
        functools.partial(crossing_kernel, count),
        out_shape=(one, one),
        in_specs=[SCALARS] + [ANYWHERE] * 4,
        out_specs=(ANYWHERE,) * 2,
        scratch_shapes=[pltpu.SemaphoreType.DMA((2,))],
        compiler_params=PARAMS,
        cost_estimate=pl.CostEstimate(flops=0, bytes_accessed=4 * moved_parts[0].size, transcendentals=0),
    )(section, *moved_parts)


def finish_kernel(
    count, core_ref, at_ref, up_own, down_own, up_got, down_got, crossed_own, crossed_got, next_ref, prev_ref, sems
):
    core, section = core_ref[0], at_ref[0]
    half = count // 2

    def put(i, src, on_down, on_up):
        @pl.when(core == 0)
        def _():
            pltpu.make_async_copy(src, on_down, sems.at[i]).start()

        @pl.when(core != 0)
        def _():
            pltpu.make_async_copy(src, on_up, sems.at[i]).start()

    places = (
        (next_ref.at[0], prev_ref.at[1]),
        (prev_ref.at[0], next_ref.at[1]),
        (prev_ref.at[1], next_ref.at[0]),
        (next_ref.at[1], prev_ref.at[0]),
    )

    @pl.when(section == half)
    def _():
        put(0, crossed_own, *places[0])
        put(2, crossed_got, *places[2])

    @pl.when(section != half)
    def _():
        put(0, up_own, *places[0])

        @pl.when(section == 0)
        def _():
            put(2, up_own, *places[2])

        @pl.when(section != 0)
        def _():
            put(2, up_got, *places[2])

    @pl.when(section == half - 1)
    def _():
        put(1, crossed_own, *places[1])
        put(3, crossed_got, *places[3])

    @pl.when(section != half - 1)
    def _():
        put(1, down_own, *places[1])

        @pl.when(section == count - 1)
        def _():
            put(3, down_own, *places[3])

        @pl.when(section != count - 1)
        def _():
            put(3, down_got, *places[3])

    for i in range(4):
        pltpu.make_async_copy(up_own, next_ref.at[0], sems.at[i]).wait()


def finish(count, core, section, *moved_parts):
    tokens, model = moved_parts[0].shape
    both = pltpu.HBM((2, tokens, model), moved_parts[0].dtype)
    return pl.pallas_call(
        functools.partial(finish_kernel, count),
        out_shape=(both, both),
        in_specs=[SCALARS] * 2 + [ANYWHERE] * 6,
        out_specs=(ANYWHERE,) * 2,
        scratch_shapes=[pltpu.SemaphoreType.DMA((4,))],
        compiler_params=PARAMS,
        cost_estimate=pl.CostEstimate(flops=0, bytes_accessed=16 * tokens * model, transcendentals=0),
    )(core, section, *moved_parts)


def add_kernel(sums_ref, partner_ref, out_ref):
    out_ref[0] = sums_ref[0] + partner_ref[1].astype(F32)
    out_ref[1] = sums_ref[1] + partner_ref[0].astype(F32)


def add_mirrored(sums, partner):
    return pl.pallas_call(
        add_kernel,
        out_shape=jax.ShapeDtypeStruct(sums.shape, F32),
        in_specs=[WHOLE] * 2,
        out_specs=WHOLE,
        compiler_params=PARAMS,
        cost_estimate=pl.CostEstimate(flops=40_000_000_000, bytes_accessed=2 << 20, transcendentals=0),
    )(sums, partner)


def moved(value, pairs, n_dp, flip=()):
    turn = n_dp // 2
    routes = [(a * n_dp + d, b * n_dp + d) for a, b in pairs for d in range(n_dp)]
    routes += [(a * n_dp + d, b * n_dp + (d ^ turn)) for a, b in flip for d in range(n_dp)]
    return lax.ppermute(value, ("section", "dp"), routes)


def shards(section_inputs, out_grads, adapters):
    n_dp = lax.axis_size("dp")
    count = lax.axis_size("section")
    half = count // 2
    core = jnp.full((1,), lax.axis_index("dp") % 2, jnp.int32)
    section = jnp.full((1,), lax.axis_index("section"), jnp.int32)
    is_down = core[0] == 0
    swap = [(i, i ^ 1) for i in range(n_dp)]
    inputs, grads = section_inputs[:, 0], out_grads[:, 0]

    gathered = lax.all_to_all(spread(adapters[:, 0], n_dp), "dp", 0, 0, tiled=True)
    given = jnp.stack([jnp.where(is_down, inputs[1], inputs[0]), jnp.where(is_down, grads[1], grads[0])])
    taken = lax.ppermute(given, "dp", swap)
    x, g, taken = (pltpu.with_memory_space_constraint(a, pltpu.HBM) for a in (inputs, grads, taken))
    parts, hidden, scaled, back = partials(core, x, g, taken, gathered)

    terms = lax.all_to_all(parts, "dp", 0, 0, tiled=True)
    sums = jnp.sum(terms.reshape((n_dp // 2, 2) + terms.shape[1:]).astype(F32), axis=0)

    up_own, down_own, send = outputs(core, x, g, taken, gathered, hidden, scaled, back)
    got = lax.ppermute(send, "dp", swap)
    up_own, down_own, got = lax.optimization_barrier((up_own, down_own, got))
    up_got, down_got = split(got)
    ups = [(i, i + 1) for i in range(count - 1) if i != half - 1]
    downs = [(i, i - 1) for i in range(1, count) if i != half]
    up_own = moved(up_own, ups, n_dp, [(half - 1, half)])
    down_own = moved(down_own, downs, n_dp, [(half, half - 1)])
    up_got = moved(up_got, ups + [(half - 1, 0)], n_dp)
    down_got = moved(down_got, downs + [(half, count - 1)], n_dp)
    narrow = sums.astype(jnp.bfloat16)
    partner = lax.ppermute(narrow, "section", [(i, count - 1 - i) for i in range(count)])
    narrow, up_own, down_own, up_got, down_got = lax.optimization_barrier((narrow, up_own, down_own, up_got, down_got))

    cross_own, cross_got = crossing(count, section, up_own, down_own, up_got, down_got)
    crossed_own = moved(cross_own, [], n_dp, [(half, half), (half - 1, half - 1)])
    crossed_got = moved(cross_got, [(0, half), (count - 1, half - 1)], n_dp)
    summed = add_mirrored(sums, partner)
    next_inputs, prev_grads = finish(
        count, core, section, up_own, down_own, up_got, down_got, crossed_own, crossed_got
    )
    return (next_inputs[:, None], prev_grads[:, None], summed[:, None])


def solution(mesh):
    in_specs = (
        P(None, "section", "dp", None),
        P(None, "section", "dp", None),
        P(None, "section", None, None, "dp"),
    )
    out_specs = (
        P(None, "section", "dp", None),
        P(None, "section", "dp", None),
        P(None, "section", None, None, "dp"),
    )
    return jax.shard_map(shards, mesh=mesh, in_specs=in_specs, out_specs=out_specs, check_vma=False)
```

```python
import functools

import jax
import jax.numpy as jnp
from jax import lax
from jax.experimental import pallas as pl
from jax.experimental.pallas import tpu as pltpu
from jax.sharding import PartitionSpec as P

WHOLE = pl.BlockSpec(memory_space=pltpu.VMEM)
ANYWHERE = pl.BlockSpec(memory_space=pl.ANY)
SCALARS = pl.BlockSpec(memory_space=pltpu.SMEM)
ACROSS = (((1,), (1,)), ((), ()))
OVER_TOKENS = (((0,), (0,)), ((), ()))
PARAMS = pltpu.CompilerParams(vmem_limit_bytes=12 << 20)
F32 = jnp.float32


def spread_kernel(w_ref, out_ref, sems):
    copies = [
        pltpu.make_async_copy(w_ref, out_ref.at[pl.ds(2 * i, 2)], sems.at[i]) for i in range(out_ref.shape[0] // 2)
    ]
    for copy in copies:
        copy.start()
    for copy in copies:
        copy.wait()


def spread(w, n_dp):
    return pl.pallas_call(
        spread_kernel,
        out_shape=pltpu.HBM((n_dp,) + w.shape[1:], w.dtype),
        in_specs=[WHOLE],
        out_specs=ANYWHERE,
        scratch_shapes=[pltpu.SemaphoreType.DMA((n_dp // 2,))],
        compiler_params=PARAMS,
        cost_estimate=pl.CostEstimate(flops=0, bytes_accessed=n_dp * w.size, transcendentals=0),
    )(w)


def fetch(core, x_ref, g_ref, taken_ref, xs, gs, sems):
    tokens, model = x_ref.shape[1:]
    chunks = sems.shape[0]
    own, others = pl.ds(0, tokens), pl.ds(tokens, tokens)
    copies = []
    for j in range(chunks):
        cols = pl.ds(j * (model // chunks), model // chunks)
        copies.append([
            pltpu.make_async_copy(x_ref.at[core, :, cols], xs.at[own, cols], sems.at[j, 0]),
            pltpu.make_async_copy(taken_ref.at[0, :, cols], xs.at[others, cols], sems.at[j, 1]),
            pltpu.make_async_copy(g_ref.at[core, :, cols], gs.at[own, cols], sems.at[j, 2]),
            pltpu.make_async_copy(taken_ref.at[1, :, cols], gs.at[others, cols], sems.at[j, 3]),
        ])
        for copy in copies[-1]:
            copy.start()
    return copies


def partials_kernel(
    core_ref, x_ref, g_ref, taken_ref, w_ref, part_ref, hidden_ref, scaled_ref, back_ref, xs, gs, ps, loads, stores
):
    slices, _, rank, width = w_ref.shape
    tokens, model = xs.shape
    chunks = loads.shape[0]
    per = slices // chunks
    fetches = fetch(core_ref[0], x_ref, g_ref, taken_ref, xs, gs, loads)

    u = jnp.zeros((tokens, rank), F32)
    v = jnp.zeros((tokens, rank), F32)
    squares = jnp.zeros((tokens, 128), F32)
    for i in range(slices):
        if i % per == 0:
            for copy in fetches[i // per]:
                copy.wait()
        cols = pl.ds(i * width, width)
        x = xs[:, cols]
        u += lax.dot_general(x, w_ref[i, 0], ACROSS, preferred_element_type=F32)
        v += lax.dot_general(gs[:, cols], w_ref[i, 1], ACROSS, preferred_element_type=F32)
        xf = x.astype(F32)
        for j in range(width // 128):
            piece = xf[:, j * 128:(j + 1) * 128]
            squares += piece * piece
    scale = lax.rsqrt(jnp.sum(squares, axis=1, keepdims=True) / model + 1e-05)
    pre = scale * u
    sig = jax.nn.sigmoid(pre)
    hidden = (pre * sig).astype(jnp.bfloat16)
    dpre = v * (sig * (1.0 + pre * (1.0 - sig)))
    inner = jnp.sum(dpre * u, axis=1, keepdims=True) / model
    scaled = (scale * dpre).astype(jnp.bfloat16)
    hidden_ref[...] = hidden
    scaled_ref[...] = scaled
    back_ref[...] = jnp.broadcast_to(inner * scale * scale * scale, back_ref.shape)

    stored = []
    for i in range(slices):
        cols = pl.ds(i * width, width)
        ps[i, 0] = lax.dot_general(scaled, xs[:, cols], OVER_TOKENS, preferred_element_type=F32).astype(ps.dtype)
        ps[i, 1] = lax.dot_general(hidden, gs[:, cols], OVER_TOKENS, preferred_element_type=F32).astype(ps.dtype)
        if i % per == per - 1:
            some = pl.ds(i + 1 - per, per)
            stored.append(pltpu.make_async_copy(ps.at[some], part_ref.at[some], stores.at[i // per]))
            stored[-1].start()
    for copy in stored:
        copy.wait()


def partials(core, x, g, taken, w):
    tokens, model, rank = 2 * x.shape[1], x.shape[2], w.shape[2]
    both = pltpu.VMEM((tokens, model), x.dtype)
    inside = jax.ShapeDtypeStruct((tokens, rank), x.dtype)
    return pl.pallas_call(
        partials_kernel,
        out_shape=(pltpu.HBM(w.shape, w.dtype), inside, inside, jax.ShapeDtypeStruct((tokens, 128), F32)),
        in_specs=[SCALARS] + [ANYWHERE] * 3 + [WHOLE],
        out_specs=(ANYWHERE,) + (WHOLE,) * 3,
        scratch_shapes=[
            both,
            both,
            pltpu.VMEM(w.shape, w.dtype),
            pltpu.SemaphoreType.DMA((4, 4)),
            pltpu.SemaphoreType.DMA((4,)),
        ],
        compiler_params=PARAMS,
        cost_estimate=pl.CostEstimate(flops=4 * tokens * w.size, bytes_accessed=8 << 20, transcendentals=0),
    )(core, x, g, taken, w)


def outputs_kernel(
    count, core_ref, at_ref, x_ref, g_ref, taken_ref, w_ref, hidden_ref, scaled_ref, back_ref, keep_ref, edge_ref,
    send_ref, xs, gs, ms, loads, stores, edge_sem
):
    core = core_ref[0]
    is_down = core == 0
    slices, _, rank, width = w_ref.shape
    tokens, model = x_ref.shape[1:]
    chunks = loads.shape[0]
    per = slices // chunks
    own, others = pl.ds(0, tokens), pl.ds(tokens, tokens)
    fetches = fetch(core, x_ref, g_ref, taken_ref, xs, gs, loads)
    hidden, scaled, back = hidden_ref[...], scaled_ref[...], back_ref[:, :1]
    stored = []
    for i in range(slices):
        if i % per == 0:
            for copy in fetches[i // per]:
                copy.wait()
        cols = pl.ds(i * width, width)
        xf, gf = xs[:, cols].astype(F32), gs[:, cols].astype(F32)
        y = (xf + jnp.dot(hidden, w_ref[i, 1], preferred_element_type=F32)).astype(ms.dtype)
        dx = (gf + jnp.dot(scaled, w_ref[i, 0], preferred_element_type=F32) - xf * back).astype(ms.dtype)
        ms[0, :, cols] = jnp.where(is_down, y, dx)
        ms[1, :, cols] = jnp.where(is_down, dx, y)
        if i % per == per - 1:
            j = i // per
            cols = pl.ds(j * (model // chunks), model // chunks)
            for copy in (
                pltpu.make_async_copy(ms.at[0, own, cols], keep_ref.at[0, :, cols], stores.at[j, 0]),
                pltpu.make_async_copy(ms.at[1, own, cols], keep_ref.at[1, :, cols], stores.at[j, 1]),
                pltpu.make_async_copy(ms.at[0, others, cols], send_ref.at[0, :, cols], stores.at[j, 2]),
                pltpu.make_async_copy(ms.at[1, others, cols], send_ref.at[1, :, cols], stores.at[j, 3]),
            ):
                copy.start()
                stored.append(copy)
    for way, position in ((0, count // 2 - 1), (1, count // 2)):
        @pl.when(at_ref[0] == position)
        def _():
            copy = pltpu.make_async_copy(ms.at[way, own], edge_ref, edge_sem)
            copy.start()
            copy.wait()
    for copy in stored:
        copy.wait()


def outputs(count, core, section, x, g, taken, w, hidden, scaled, back):
    tokens, model = x.shape[1:]
    pair = pltpu.HBM((2, tokens, model), x.dtype)
    both = pltpu.VMEM((2 * tokens, model), x.dtype)
    return pl.pallas_call(
        functools.partial(outputs_kernel, count),
        out_shape=(pair, pltpu.HBM((tokens, model), x.dtype), pair),
        in_specs=[SCALARS] * 2 + [ANYWHERE] * 3 + [WHOLE] * 4,
        out_specs=(ANYWHERE,) * 3,
        scratch_shapes=[
            both,
            both,
            pltpu.VMEM((2, 2 * tokens, model), x.dtype),
            pltpu.SemaphoreType.DMA((4, 4)),
            pltpu.SemaphoreType.DMA((4, 4)),
            pltpu.SemaphoreType.DMA,
        ],
        compiler_params=PARAMS,
        cost_estimate=pl.CostEstimate(flops=4 * tokens * w.size, bytes_accessed=8 << 20, transcendentals=0),
    )(core, section, x, g, taken, w, hidden, scaled, back)


def pack_kernel(count, at_ref, keep_ref, got_ref, up_ref, down_ref, edge_ref, sems):
    copies = [
        pltpu.make_async_copy(keep_ref.at[0], up_ref.at[0], sems.at[0]),
        pltpu.make_async_copy(got_ref.at[0], up_ref.at[1], sems.at[1]),
        pltpu.make_async_copy(keep_ref.at[1], down_ref.at[0], sems.at[2]),
        pltpu.make_async_copy(got_ref.at[1], down_ref.at[1], sems.at[3]),
    ]
    for copy in copies:
        copy.start()
    for way, position in ((0, count // 2 - 1), (1, count // 2)):
        @pl.when(at_ref[0] == position)
        def _():
            copy = pltpu.make_async_copy(got_ref.at[way], edge_ref, sems.at[4])
            copy.start()
            copy.wait()
    for copy in copies:
        copy.wait()


def pack(count, section, keep, got):
    pair = pltpu.HBM(keep.shape, keep.dtype)
    return pl.pallas_call(
        functools.partial(pack_kernel, count),
        out_shape=(pair, pair, pltpu.HBM(keep.shape[1:], keep.dtype)),
        in_specs=[SCALARS] + [ANYWHERE] * 2,
        out_specs=(ANYWHERE,) * 3,
        scratch_shapes=[pltpu.SemaphoreType.DMA((5,))],
        compiler_params=PARAMS,
        cost_estimate=pl.CostEstimate(flops=0, bytes_accessed=8 * keep.size, transcendentals=0),
    )(section, keep, got)


def finish_kernel(
    count, core_ref, at_ref, up_ref, down_ref, crossed_own, crossed_got, next_ref, prev_ref, sems
):
    core, section = core_ref[0], at_ref[0]
    half = count // 2

    def put(i, src, on_down, on_up):
        @pl.when(core == 0)
        def _():
            pltpu.make_async_copy(src, on_down, sems.at[i]).start()

        @pl.when(core != 0)
        def _():
            pltpu.make_async_copy(src, on_up, sems.at[i]).start()

    places = (
        (next_ref.at[0], prev_ref.at[1]),
        (prev_ref.at[0], next_ref.at[1]),
        (prev_ref.at[1], next_ref.at[0]),
        (next_ref.at[1], prev_ref.at[0]),
    )
    for way, position, arrived in ((0, half, up_ref), (1, half - 1, down_ref)):
        @pl.when(section == position)
        def _():
            put(way, crossed_own, *places[way])
            put(way + 2, crossed_got, *places[way + 2])

        @pl.when(section != position)
        def _():
            put(way, arrived.at[0], *places[way])
            put(way + 2, arrived.at[1], *places[way + 2])

    for i in range(4):
        pltpu.make_async_copy(crossed_own, next_ref.at[0], sems.at[i]).wait()


def finish(count, core, section, up, down, crossed_own, crossed_got):
    pair = pltpu.HBM(up.shape, up.dtype)
    return pl.pallas_call(
        functools.partial(finish_kernel, count),
        out_shape=(pair, pair),
        in_specs=[SCALARS] * 2 + [ANYWHERE] * 4,
        out_specs=(ANYWHERE,) * 2,
        scratch_shapes=[pltpu.SemaphoreType.DMA((4,))],
        compiler_params=PARAMS,
        cost_estimate=pl.CostEstimate(flops=0, bytes_accessed=8 * up.size, transcendentals=0),
    )(core, section, up, down, crossed_own, crossed_got)


def add_kernel(sums_ref, partner_ref, out_ref):
    out_ref[0] = sums_ref[0] + partner_ref[1].astype(F32)
    out_ref[1] = sums_ref[1] + partner_ref[0].astype(F32)


def add_mirrored(sums, partner):
    return pl.pallas_call(
        add_kernel,
        out_shape=jax.ShapeDtypeStruct(sums.shape, F32),
        in_specs=[WHOLE] * 2,
        out_specs=WHOLE,
        compiler_params=PARAMS,
        cost_estimate=pl.CostEstimate(flops=4_000_000_000, bytes_accessed=2 << 20, transcendentals=0),
    )(sums, partner)


def moved(value, pairs, n_dp, flip=()):
    turn = n_dp // 2
    routes = [(a * n_dp + d, b * n_dp + d) for a, b in pairs for d in range(n_dp)]
    routes += [(a * n_dp + d, b * n_dp + (d ^ turn)) for a, b in flip for d in range(n_dp)]
    return lax.ppermute(value, ("section", "dp"), routes)


def shards(section_inputs, out_grads, adapters):
    n_dp = lax.axis_size("dp")
    count = lax.axis_size("section")
    half = count // 2
    core = jnp.full((1,), lax.axis_index("dp") % 2, jnp.int32)
    section = jnp.full((1,), lax.axis_index("section"), jnp.int32)
    is_down = core[0] == 0
    swap = [(i, i ^ 1) for i in range(n_dp)]
    inputs, grads = section_inputs[:, 0], out_grads[:, 0]

    gathered = lax.all_to_all(spread(adapters[:, 0], n_dp), "dp", 0, 0, tiled=True)
    given = jnp.stack([jnp.where(is_down, inputs[1], inputs[0]), jnp.where(is_down, grads[1], grads[0])])
    taken = lax.ppermute(given, "dp", swap)
    x, g, taken = (pltpu.with_memory_space_constraint(a, pltpu.HBM) for a in (inputs, grads, taken))
    parts, hidden, scaled, back = partials(core, x, g, taken, gathered)

    terms = lax.all_to_all(parts, "dp", 0, 0, tiled=True)
    sums = jnp.sum(terms.reshape((n_dp // 2, 2) + terms.shape[1:]).astype(F32), axis=0)

    keep, edge_own, send = outputs(count, core, section, x, g, taken, gathered, hidden, scaled, back)
    got = lax.ppermute(send, "dp", swap)
    up, down, edge_got = pack(count, section, keep, got)
    near_own = moved(edge_own, [], n_dp, [(half - 1, half), (half, half - 1)])
    near_got = moved(edge_got, [(half - 1, 0), (half, count - 1)], n_dp)
    up = moved(up, [(i, i + 1) for i in range(count - 1) if i != half - 1], n_dp)
    down = moved(down, [(i, i - 1) for i in range(1, count) if i != half], n_dp)

    narrow = sums.astype(jnp.bfloat16)
    partner = lax.ppermute(narrow, "section", [(i, count - 1 - i) for i in range(count)])
    narrow, near_own, near_got = lax.optimization_barrier((narrow, near_own, near_got))
    crossed_own = moved(near_own, [], n_dp, [(half, half), (half - 1, half - 1)])
    crossed_got = moved(near_got, [(0, half), (count - 1, half - 1)], n_dp)
    summed = add_mirrored(sums, partner)
    next_inputs, prev_grads = finish(count, core, section, up, down, crossed_own, crossed_got)
    return (next_inputs[:, None], prev_grads[:, None], summed[:, None])


def solution(mesh):
    in_specs = (
        P(None, "section", "dp", None),
        P(None, "section", "dp", None),
        P(None, "section", None, None, "dp"),
    )
    out_specs = (
        P(None, "section", "dp", None),
        P(None, "section", "dp", None),
        P(None, "section", None, None, "dp"),
    )
    return jax.shard_map(shards, mesh=mesh, in_specs=in_specs, out_specs=out_specs, check_vma=False)
```

```python
import functools

import jax
import jax.numpy as jnp
from jax import lax
from jax.experimental import pallas as pl
from jax.experimental.pallas import tpu as pltpu
from jax.sharding import PartitionSpec as P

WHOLE = pl.BlockSpec(memory_space=pltpu.VMEM)
ANYWHERE = pl.BlockSpec(memory_space=pl.ANY)
SCALARS = pl.BlockSpec(memory_space=pltpu.SMEM)
ACROSS = (((1,), (1,)), ((), ()))
OVER_TOKENS = (((0,), (0,)), ((), ()))
PARAMS = pltpu.CompilerParams(vmem_limit_bytes=12 << 20)
F32 = jnp.float32


def spread_kernel(w_ref, out_ref, sems):
    copies = [
        pltpu.make_async_copy(w_ref, out_ref.at[pl.ds(2 * i, 2)], sems.at[i]) for i in range(out_ref.shape[0] // 2)
    ]
    for copy in copies:
        copy.start()
    for copy in copies:
        copy.wait()


def spread(w, n_dp):
    return pl.pallas_call(
        spread_kernel,
        out_shape=pltpu.HBM((n_dp,) + w.shape[1:], w.dtype),
        in_specs=[WHOLE],
        out_specs=ANYWHERE,
        scratch_shapes=[pltpu.SemaphoreType.DMA((n_dp // 2,))],
        compiler_params=PARAMS,
        cost_estimate=pl.CostEstimate(flops=0, bytes_accessed=n_dp * w.size, transcendentals=0),
    )(w)


def fetch(core, x_ref, g_ref, taken_ref, xs, gs, sems):
    tokens, model = x_ref.shape[1:]
    chunks = sems.shape[0]
    own, others = pl.ds(0, tokens), pl.ds(tokens, tokens)
    copies = []
    for j in range(chunks):
        cols = pl.ds(j * (model // chunks), model // chunks)
        copies.append([
            pltpu.make_async_copy(x_ref.at[core, :, cols], xs.at[own, cols], sems.at[j, 0]),
            pltpu.make_async_copy(taken_ref.at[0, :, cols], xs.at[others, cols], sems.at[j, 1]),
            pltpu.make_async_copy(g_ref.at[core, :, cols], gs.at[own, cols], sems.at[j, 2]),
            pltpu.make_async_copy(taken_ref.at[1, :, cols], gs.at[others, cols], sems.at[j, 3]),
        ])
        for copy in copies[-1]:
            copy.start()
    return copies


def adapter_kernel(
    count, core_ref, at_ref, x_ref, g_ref, taken_ref, w_ref, part_ref, up_ref, down_ref, up_send, down_send, edge_ref,
    xs, gs, ps, ms, loads, part_stores, stores, edge_sem
):
    is_down = core_ref[0] == 0
    slices, _, rank, width = w_ref.shape
    tokens, model = up_ref.shape
    chunks = loads.shape[0]
    per = slices // chunks
    own, others = pl.ds(0, tokens), pl.ds(tokens, tokens)
    fetches = fetch(core_ref[0], x_ref, g_ref, taken_ref, xs, gs, loads)

    u = jnp.zeros((2 * tokens, rank), F32)
    v = jnp.zeros((2 * tokens, rank), F32)
    squares = jnp.zeros((2 * tokens, 128), F32)
    for i in range(slices):
        if i % per == 0:
            for copy in fetches[i // per]:
                copy.wait()
        cols = pl.ds(i * width, width)
        x = xs[:, cols]
        u += lax.dot_general(x, w_ref[i, 0], ACROSS, preferred_element_type=F32)
        v += lax.dot_general(gs[:, cols], w_ref[i, 1], ACROSS, preferred_element_type=F32)
        xf = x.astype(F32)
        for j in range(width // 128):
            piece = xf[:, j * 128:(j + 1) * 128]
            squares += piece * piece
    scale = lax.rsqrt(jnp.sum(squares, axis=1, keepdims=True) / model + 1e-05)
    pre = scale * u
    sig = jax.nn.sigmoid(pre)
    hidden = (pre * sig).astype(jnp.bfloat16)
    dpre = v * (sig * (1.0 + pre * (1.0 - sig)))
    inner = jnp.sum(dpre * u, axis=1, keepdims=True) / model
    scaled = (scale * dpre).astype(jnp.bfloat16)
    back = inner * scale * scale * scale

    stored = []
    for i in range(slices):
        cols = pl.ds(i * width, width)
        ps[i, 0] = lax.dot_general(scaled, xs[:, cols], OVER_TOKENS, preferred_element_type=F32).astype(ps.dtype)
        ps[i, 1] = lax.dot_general(hidden, gs[:, cols], OVER_TOKENS, preferred_element_type=F32).astype(ps.dtype)
        xf, gf = xs[:, cols].astype(F32), gs[:, cols].astype(F32)
        y = (xf + jnp.dot(hidden, w_ref[i, 1], preferred_element_type=F32)).astype(ms.dtype)
        dx = (gf + jnp.dot(scaled, w_ref[i, 0], preferred_element_type=F32) - xf * back).astype(ms.dtype)
        ms[0, :, cols] = jnp.where(is_down, y, dx)
        ms[1, :, cols] = jnp.where(is_down, dx, y)
        if i % per == per - 1:
            j = i // per
            some = pl.ds(j * per, per)
            cols = pl.ds(j * (model // chunks), model // chunks)
            for copy in (
                pltpu.make_async_copy(ps.at[some], part_ref.at[some], part_stores.at[j]),
                pltpu.make_async_copy(ms.at[0, own, cols], up_ref.at[:, cols], stores.at[j, 0]),
                pltpu.make_async_copy(ms.at[1, own, cols], down_ref.at[:, cols], stores.at[j, 1]),
                pltpu.make_async_copy(ms.at[0, others, cols], up_send.at[:, cols], stores.at[j, 2]),
                pltpu.make_async_copy(ms.at[1, others, cols], down_send.at[:, cols], stores.at[j, 3]),
            ):
                copy.start()
                stored.append(copy)
    for way, position in ((0, count // 2 - 1), (1, count // 2)):
        @pl.when(at_ref[0] == position)
        def _():
            copy = pltpu.make_async_copy(ms.at[way, others], edge_ref, edge_sem)
            copy.start()
            copy.wait()
    for copy in stored:
        copy.wait()


def adapter(count, core, section, x, g, taken, w):
    tokens, model = x.shape[1:]
    one = pltpu.HBM((tokens, model), x.dtype)
    both = pltpu.VMEM((2 * tokens, model), x.dtype)
    return pl.pallas_call(
        functools.partial(adapter_kernel, count),
        out_shape=(pltpu.HBM(w.shape, w.dtype),) + (one,) * 5,
        in_specs=[SCALARS] * 2 + [ANYWHERE] * 3 + [WHOLE],
        out_specs=(ANYWHERE,) * 6,
        scratch_shapes=[
            both,
            both,
            pltpu.VMEM(w.shape, w.dtype),
            pltpu.VMEM((2, 2 * tokens, model), x.dtype),
            pltpu.SemaphoreType.DMA((4, 4)),
            pltpu.SemaphoreType.DMA((4,)),
            pltpu.SemaphoreType.DMA((4, 4)),
            pltpu.SemaphoreType.DMA,
        ],
        compiler_params=PARAMS,
        cost_estimate=pl.CostEstimate(flops=12 * tokens * w.size, bytes_accessed=12 << 20, transcendentals=0),
    )(core, section, x, g, taken, w)


def crossing_kernel(count, at_ref, up_ref, down_ref, out_ref, sem):
    for arrived, position in ((up_ref, count // 2), (down_ref, count // 2 - 1)):
        @pl.when(at_ref[0] == position)
        def _():
            copy = pltpu.make_async_copy(arrived, out_ref, sem)
            copy.start()
            copy.wait()


def crossing(count, section, up, down):
    return pl.pallas_call(
        functools.partial(crossing_kernel, count),
        out_shape=pltpu.HBM(up.shape, up.dtype),
        in_specs=[SCALARS] + [ANYWHERE] * 2,
        out_specs=ANYWHERE,
        scratch_shapes=[pltpu.SemaphoreType.DMA],
        compiler_params=PARAMS,
        cost_estimate=pl.CostEstimate(flops=0, bytes_accessed=4 * up.size, transcendentals=0),
    )(section, up, down)


def finish_kernel(
    count, core_ref, at_ref, up_own, down_own, up_got, down_got, crossed_own, crossed_got, next_ref, prev_ref, sems
):
    core, section = core_ref[0], at_ref[0]
    half = count // 2

    def put(i, src, on_down, on_up):
        @pl.when(core == 0)
        def _():
            pltpu.make_async_copy(src, on_down, sems.at[i]).start()

        @pl.when(core != 0)
        def _():
            pltpu.make_async_copy(src, on_up, sems.at[i]).start()

    places = (
        (next_ref.at[0], prev_ref.at[1]),
        (prev_ref.at[0], next_ref.at[1]),
        (prev_ref.at[1], next_ref.at[0]),
        (next_ref.at[1], prev_ref.at[0]),
    )
    for way, position, own, got in ((0, half, up_own, up_got), (1, half - 1, down_own, down_got)):
        @pl.when(section == position)
        def _():
            put(way, crossed_own, *places[way])
            put(way + 2, crossed_got, *places[way + 2])

        @pl.when(section != position)
        def _():
            put(way, own, *places[way])
            put(way + 2, got, *places[way + 2])

    for i in range(4):
        pltpu.make_async_copy(crossed_own, next_ref.at[0], sems.at[i]).wait()


def finish(count, core, section, *arrived):
    tokens, model = arrived[0].shape
    pair = pltpu.HBM((2, tokens, model), arrived[0].dtype)
    return pl.pallas_call(
        functools.partial(finish_kernel, count),
        out_shape=(pair, pair),
        in_specs=[SCALARS] * 2 + [ANYWHERE] * 6,
        out_specs=(ANYWHERE,) * 2,
        scratch_shapes=[pltpu.SemaphoreType.DMA((4,))],
        compiler_params=PARAMS,
        cost_estimate=pl.CostEstimate(flops=0, bytes_accessed=16 * tokens * model, transcendentals=0),
    )(core, section, *arrived)


def add_kernel(sums_ref, partner_ref, out_ref):
    out_ref[0] = sums_ref[0] + partner_ref[1].astype(F32)
    out_ref[1] = sums_ref[1] + partner_ref[0].astype(F32)


def add_mirrored(sums, partner):
    return pl.pallas_call(
        add_kernel,
        out_shape=jax.ShapeDtypeStruct(sums.shape, F32),
        in_specs=[WHOLE] * 2,
        out_specs=WHOLE,
        compiler_params=PARAMS,
        cost_estimate=pl.CostEstimate(flops=4_000_000_000, bytes_accessed=2 << 20, transcendentals=0),
    )(sums, partner)


def moved(value, routes, n_dp):
    pairs = [(a * n_dp + d, b * n_dp + (d ^ turn)) for a, b, turn in routes for d in range(n_dp)]
    return lax.ppermute(value, ("section", "dp"), pairs)


def shards(section_inputs, out_grads, adapters):
    n_dp = lax.axis_size("dp")
    count = lax.axis_size("section")
    half = count // 2
    core = jnp.full((1,), lax.axis_index("dp") % 2, jnp.int32)
    section = jnp.full((1,), lax.axis_index("section"), jnp.int32)
    is_down = core[0] == 0
    swap = [(i, i ^ 1) for i in range(n_dp)]
    inputs, grads = section_inputs[:, 0], out_grads[:, 0]

    gathered = lax.all_to_all(spread(adapters[:, 0], n_dp), "dp", 0, 0, tiled=True)
    given = jnp.stack([jnp.where(is_down, inputs[1], inputs[0]), jnp.where(is_down, grads[1], grads[0])])
    taken = lax.ppermute(given, "dp", swap)
    x, g, taken = (pltpu.with_memory_space_constraint(a, pltpu.HBM) for a in (inputs, grads, taken))
    parts, up_own, down_own, up_send, down_send, edge = adapter(count, core, section, x, g, taken, gathered)

    terms = lax.all_to_all(parts, "dp", 0, 0, tiled=True)
    sums = jnp.sum(terms.reshape((n_dp // 2, 2) + terms.shape[1:]).astype(F32), axis=0)

    group = n_dp // 2
    ups = [(i, i + 1) for i in range(count - 1) if i != half - 1]
    downs = [(i, i - 1) for i in range(1, count) if i != half]
    up_own = moved(up_own, [(a, b, 0) for a, b in ups] + [(half - 1, half, group)], n_dp)
    down_own = moved(down_own, [(a, b, 0) for a, b in downs] + [(half, half - 1, group)], n_dp)
    near = moved(edge, [(half - 1, 0, 1), (half, count - 1, 1)], n_dp)
    up_got = moved(up_send, [(a, b, 1) for a, b in ups], n_dp)
    down_got = moved(down_send, [(a, b, 1) for a, b in downs], n_dp)

    narrow = sums.astype(jnp.bfloat16)
    narrow, up_own, down_own, up_got, down_got = lax.optimization_barrier((narrow, up_own, down_own, up_got, down_got))
    partner = lax.ppermute(narrow, "section", [(i, count - 1 - i) for i in range(count)])
    crossed_own = moved(crossing(count, section, up_own, down_own), [(half, half, group), (half - 1, half - 1, group)], n_dp)
    crossed_got = moved(near, [(0, half, 0), (count - 1, half - 1, 0)], n_dp)
    summed = add_mirrored(sums, partner)
    next_inputs, prev_grads = finish(
        count, core, section, up_own, down_own, up_got, down_got, crossed_own, crossed_got
    )
    return (next_inputs[:, None], prev_grads[:, None], summed[:, None])


def solution(mesh):
    in_specs = (
        P(None, "section", "dp", None),
        P(None, "section", "dp", None),
        P(None, "section", None, None, "dp"),
    )
    out_specs = (
        P(None, "section", "dp", None),
        P(None, "section", "dp", None),
        P(None, "section", None, None, "dp"),
    )
    return jax.shard_map(shards, mesh=mesh, in_specs=in_specs, out_specs=out_specs, check_vma=False)
```

```python
import functools

import jax
import jax.numpy as jnp
from jax import lax
from jax.experimental import pallas as pl
from jax.experimental.pallas import tpu as pltpu
from jax.sharding import PartitionSpec as P

WHOLE = pl.BlockSpec(memory_space=pltpu.VMEM)
ANYWHERE = pl.BlockSpec(memory_space=pl.ANY)
SCALARS = pl.BlockSpec(memory_space=pltpu.SMEM)
ACROSS = (((1,), (1,)), ((), ()))
OVER_TOKENS = (((0,), (0,)), ((), ()))
PARAMS = pltpu.CompilerParams(vmem_limit_bytes=12 << 20)
F32 = jnp.float32


def in_hbm(array):
    return pltpu.with_memory_space_constraint(array, pltpu.HBM)


def spread_kernel(w_ref, out_ref, sems):
    copies = [
        pltpu.make_async_copy(w_ref, out_ref.at[pl.ds(2 * i, 2)], sems.at[i]) for i in range(out_ref.shape[0] // 2)
    ]
    for copy in copies:
        copy.start()
    for copy in copies:
        copy.wait()


def spread(w, n_dp):
    return pl.pallas_call(
        spread_kernel,
        out_shape=pltpu.HBM((n_dp,) + w.shape[1:], w.dtype),
        in_specs=[ANYWHERE],
        out_specs=ANYWHERE,
        scratch_shapes=[pltpu.SemaphoreType.DMA((n_dp // 2,))],
        compiler_params=PARAMS,
        cost_estimate=pl.CostEstimate(flops=0, bytes_accessed=n_dp * w.size, transcendentals=0),
    )(in_hbm(w))


def fetch(core, x_ref, g_ref, taken_ref, xs, gs, sems):
    tokens, model = x_ref.shape[1:]
    chunks = sems.shape[0]
    own, others = pl.ds(0, tokens), pl.ds(tokens, tokens)
    copies = []
    for j in range(chunks):
        cols = pl.ds(j * (model // chunks), model // chunks)
        copies.append([
            pltpu.make_async_copy(x_ref.at[core, :, cols], xs.at[own, cols], sems.at[j, 0]),
            pltpu.make_async_copy(taken_ref.at[0, :, cols], xs.at[others, cols], sems.at[j, 1]),
            pltpu.make_async_copy(g_ref.at[core, :, cols], gs.at[own, cols], sems.at[j, 2]),
            pltpu.make_async_copy(taken_ref.at[1, :, cols], gs.at[others, cols], sems.at[j, 3]),
        ])
        for copy in copies[-1]:
            copy.start()
    return copies


def adapter_kernel(
    count, core_ref, at_ref, x_ref, g_ref, taken_ref, w_ref, part_ref, up_ref, down_ref, up_send, down_send, edge_ref,
    xs, gs, ps, ms, loads, part_stores, stores, edge_sem
):
    is_down = core_ref[0] == 0
    slices, _, rank, width = w_ref.shape
    tokens, model = up_ref.shape
    chunks = loads.shape[0]
    per = slices // chunks
    own, others = pl.ds(0, tokens), pl.ds(tokens, tokens)
    fetches = fetch(core_ref[0], x_ref, g_ref, taken_ref, xs, gs, loads)

    u = jnp.zeros((2 * tokens, rank), F32)
    v = jnp.zeros((2 * tokens, rank), F32)
    squares = jnp.zeros((2 * tokens, 128), F32)
    for i in range(slices):
        if i % per == 0:
            for copy in fetches[i // per]:
                copy.wait()
        cols = pl.ds(i * width, width)
        x = xs[:, cols]
        u += lax.dot_general(x, w_ref[i, 0], ACROSS, preferred_element_type=F32)
        v += lax.dot_general(gs[:, cols], w_ref[i, 1], ACROSS, preferred_element_type=F32)
        xf = x.astype(F32)
        for j in range(width // 128):
            piece = xf[:, j * 128:(j + 1) * 128]
            squares += piece * piece
    scale = lax.rsqrt(jnp.sum(squares, axis=1, keepdims=True) / model + 1e-05)
    pre = scale * u
    sig = jax.nn.sigmoid(pre)
    hidden = (pre * sig).astype(jnp.bfloat16)
    dpre = v * (sig * (1.0 + pre * (1.0 - sig)))
    inner = jnp.sum(dpre * u, axis=1, keepdims=True) / model
    scaled = (scale * dpre).astype(jnp.bfloat16)
    back = inner * scale * scale * scale

    stored = []
    for i in range(slices):
        cols = pl.ds(i * width, width)
        ps[i, 0] = lax.dot_general(scaled, xs[:, cols], OVER_TOKENS, preferred_element_type=F32).astype(ps.dtype)
        ps[i, 1] = lax.dot_general(hidden, gs[:, cols], OVER_TOKENS, preferred_element_type=F32).astype(ps.dtype)
        xf, gf = xs[:, cols].astype(F32), gs[:, cols].astype(F32)
        y = (xf + jnp.dot(hidden, w_ref[i, 1], preferred_element_type=F32)).astype(ms.dtype)
        dx = (gf + jnp.dot(scaled, w_ref[i, 0], preferred_element_type=F32) - xf * back).astype(ms.dtype)
        ms[0, :, cols] = jnp.where(is_down, y, dx)
        ms[1, :, cols] = jnp.where(is_down, dx, y)
        if i % per == per - 1:
            j = i // per
            some = pl.ds(j * per, per)
            cols = pl.ds(j * (model // chunks), model // chunks)
            for copy in (
                pltpu.make_async_copy(ps.at[some], part_ref.at[some], part_stores.at[j]),
                pltpu.make_async_copy(ms.at[0, own, cols], up_ref.at[:, cols], stores.at[j, 0]),
                pltpu.make_async_copy(ms.at[1, own, cols], down_ref.at[:, cols], stores.at[j, 1]),
                pltpu.make_async_copy(ms.at[0, others, cols], up_send.at[:, cols], stores.at[j, 2]),
                pltpu.make_async_copy(ms.at[1, others, cols], down_send.at[:, cols], stores.at[j, 3]),
            ):
                copy.start()
                stored.append(copy)
    for way, position in ((0, count // 2 - 1), (1, count // 2)):
        @pl.when(at_ref[0] == position)
        def _():
            copy = pltpu.make_async_copy(ms.at[way, others], edge_ref, edge_sem)
            copy.start()
            copy.wait()
    for copy in stored:
        copy.wait()


def adapter(count, core, section, x, g, taken, w):
    tokens, model = x.shape[1:]
    one = pltpu.HBM((tokens, model), x.dtype)
    both = pltpu.VMEM((2 * tokens, model), x.dtype)
    return pl.pallas_call(
        functools.partial(adapter_kernel, count),
        out_shape=(pltpu.HBM(w.shape, w.dtype),) + (one,) * 5,
        in_specs=[SCALARS] * 2 + [ANYWHERE] * 3 + [WHOLE],
        out_specs=(ANYWHERE,) * 6,
        scratch_shapes=[
            both,
            both,
            pltpu.VMEM(w.shape, w.dtype),
            pltpu.VMEM((2, 2 * tokens, model), x.dtype),
            pltpu.SemaphoreType.DMA((8, 4)),
            pltpu.SemaphoreType.DMA((8,)),
            pltpu.SemaphoreType.DMA((8, 4)),
            pltpu.SemaphoreType.DMA,
        ],
        compiler_params=PARAMS,
        cost_estimate=pl.CostEstimate(flops=12 * tokens * w.size, bytes_accessed=12 << 20, transcendentals=0),
    )(core, section, x, g, taken, w)


def crossing_kernel(count, at_ref, up_ref, down_ref, out_ref, sem):
    for arrived, position in ((up_ref, count // 2), (down_ref, count // 2 - 1)):
        @pl.when(at_ref[0] == position)
        def _():
            copy = pltpu.make_async_copy(arrived, out_ref, sem)
            copy.start()
            copy.wait()


def crossing(count, section, up, down):
    return pl.pallas_call(
        functools.partial(crossing_kernel, count),
        out_shape=pltpu.HBM(up.shape, up.dtype),
        in_specs=[SCALARS] + [ANYWHERE] * 2,
        out_specs=ANYWHERE,
        scratch_shapes=[pltpu.SemaphoreType.DMA],
        compiler_params=PARAMS,
        cost_estimate=pl.CostEstimate(flops=0, bytes_accessed=4 * up.size, transcendentals=0),
    )(section, up, down)


def finish_kernel(
    count, core_ref, at_ref, up_own, down_own, up_got, down_got, crossed_own, crossed_got, next_ref, prev_ref, sems
):
    core, section = core_ref[0], at_ref[0]
    half = count // 2

    def put(i, src, on_down, on_up):
        @pl.when(core == 0)
        def _():
            pltpu.make_async_copy(src, on_down, sems.at[i]).start()

        @pl.when(core != 0)
        def _():
            pltpu.make_async_copy(src, on_up, sems.at[i]).start()

    places = (
        (next_ref.at[0], prev_ref.at[1]),
        (prev_ref.at[0], next_ref.at[1]),
        (prev_ref.at[1], next_ref.at[0]),
        (next_ref.at[1], prev_ref.at[0]),
    )
    for way, position, own, got in ((0, half, up_own, up_got), (1, half - 1, down_own, down_got)):
        @pl.when(section == position)
        def _():
            put(way, crossed_own, *places[way])
            put(way + 2, crossed_got, *places[way + 2])

        @pl.when(section != position)
        def _():
            put(way, own, *places[way])
            put(way + 2, got, *places[way + 2])

    for i in range(4):
        pltpu.make_async_copy(crossed_own, next_ref.at[0], sems.at[i]).wait()


def finish(count, core, section, *arrived):
    tokens, model = arrived[0].shape
    pair = pltpu.HBM((2, tokens, model), arrived[0].dtype)
    return pl.pallas_call(
        functools.partial(finish_kernel, count),
        out_shape=(pair, pair),
        in_specs=[SCALARS] * 2 + [ANYWHERE] * 6,
        out_specs=(ANYWHERE,) * 2,
        scratch_shapes=[pltpu.SemaphoreType.DMA((4,))],
        compiler_params=PARAMS,
        cost_estimate=pl.CostEstimate(flops=0, bytes_accessed=16 * tokens * model, transcendentals=0),
    )(core, section, *arrived[:2], *(in_hbm(a) for a in arrived[2:4]), *arrived[4:])


def add_kernel(sums_ref, partner_ref, out_ref):
    out_ref[0] = sums_ref[0] + partner_ref[1].astype(F32)
    out_ref[1] = sums_ref[1] + partner_ref[0].astype(F32)


def add_mirrored(sums, partner):
    return pl.pallas_call(
        add_kernel,
        out_shape=jax.ShapeDtypeStruct(sums.shape, F32),
        in_specs=[WHOLE] * 2,
        out_specs=WHOLE,
        compiler_params=PARAMS,
        cost_estimate=pl.CostEstimate(flops=4_000_000_000, bytes_accessed=2 << 20, transcendentals=0),
    )(sums, partner)


def moved(value, routes, n_dp):
    pairs = [(a * n_dp + d, b * n_dp + (d ^ turn)) for a, b, turn in routes for d in range(n_dp)]
    return lax.ppermute(value, ("section", "dp"), pairs)


def shards(section_inputs, out_grads, adapters):
    n_dp = lax.axis_size("dp")
    count = lax.axis_size("section")
    half = count // 2
    core = jnp.full((1,), lax.axis_index("dp") % 2, jnp.int32)
    section = jnp.full((1,), lax.axis_index("section"), jnp.int32)
    is_down = core[0] == 0
    swap = [(i, i ^ 1) for i in range(n_dp)]
    inputs, grads = section_inputs[:, 0], out_grads[:, 0]

    gathered = lax.all_to_all(spread(adapters[:, 0], n_dp), "dp", 0, 0, tiled=True)
    given = jnp.stack([jnp.where(is_down, inputs[1], inputs[0]), jnp.where(is_down, grads[1], grads[0])])
    taken = lax.ppermute(given, "dp", swap)
    x, g, taken = (in_hbm(a) for a in (inputs, grads, taken))
    parts, up_own, down_own, up_send, down_send, edge = adapter(count, core, section, x, g, taken, gathered)

    terms = lax.all_to_all(parts, "dp", 0, 0, tiled=True)
    sums = jnp.sum(terms.reshape((n_dp // 2, 2) + terms.shape[1:]).astype(F32), axis=0)

    group = n_dp // 2
    ups = [(i, i + 1) for i in range(count - 1) if i != half - 1]
    downs = [(i, i - 1) for i in range(1, count) if i != half]
    up_own = moved(up_own, [(a, b, 0) for a, b in ups] + [(half - 1, half, group)], n_dp)
    down_own = moved(down_own, [(a, b, 0) for a, b in downs] + [(half, half - 1, group)], n_dp)
    near = moved(edge, [(half - 1, 0, 1), (half, count - 1, 1)], n_dp)
    up_got = moved(up_send, [(a, b, 1) for a, b in ups], n_dp)
    down_got = moved(down_send, [(a, b, 1) for a, b in downs], n_dp)

    narrow = sums.astype(jnp.bfloat16)
    narrow, up_own, down_own, up_got, down_got = lax.optimization_barrier((narrow, up_own, down_own, up_got, down_got))
    partner = lax.ppermute(narrow, "section", [(i, count - 1 - i) for i in range(count)])
    crossed_own = moved(crossing(count, section, up_own, down_own), [(half, half, group), (half - 1, half - 1, group)], n_dp)
    crossed_got = moved(near, [(0, half, 0), (count - 1, half - 1, 0)], n_dp)
    summed = add_mirrored(sums, partner)
    next_inputs, prev_grads = finish(
        count, core, section, up_own, down_own, up_got, down_got, crossed_own, crossed_got
    )
    return (next_inputs[:, None], prev_grads[:, None], summed[:, None])


def solution(mesh):
    in_specs = (
        P(None, "section", "dp", None),
        P(None, "section", "dp", None),
        P(None, "section", None, None, "dp"),
    )
    out_specs = (
        P(None, "section", "dp", None),
        P(None, "section", "dp", None),
        P(None, "section", None, None, "dp"),
    )
    return jax.shard_map(shards, mesh=mesh, in_specs=in_specs, out_specs=out_specs, check_vma=False)
```

```python
import functools

import jax
import jax.numpy as jnp
from jax import lax
from jax.experimental import pallas as pl
from jax.experimental.pallas import tpu as pltpu
from jax.sharding import PartitionSpec as P

WHOLE = pl.BlockSpec(memory_space=pltpu.VMEM)
ANYWHERE = pl.BlockSpec(memory_space=pl.ANY)
SCALARS = pl.BlockSpec(memory_space=pltpu.SMEM)
ACROSS = (((1,), (1,)), ((), ()))
OVER_TOKENS = (((0,), (0,)), ((), ()))
PARAMS = pltpu.CompilerParams(vmem_limit_bytes=12 << 20)
F32 = jnp.float32


def in_hbm(array):
    return pltpu.with_memory_space_constraint(array, pltpu.HBM)


def spread_kernel(w_ref, out_ref, sems):
    copies = [
        pltpu.make_async_copy(w_ref, out_ref.at[pl.ds(2 * i, 2)], sems.at[i]) for i in range(out_ref.shape[0] // 2)
    ]
    for copy in copies:
        copy.start()
    for copy in copies:
        copy.wait()


def spread(w, n_dp):
    return pl.pallas_call(
        spread_kernel,
        out_shape=pltpu.HBM((n_dp,) + w.shape[1:], w.dtype),
        in_specs=[WHOLE],
        out_specs=ANYWHERE,
        scratch_shapes=[pltpu.SemaphoreType.DMA((n_dp // 2,))],
        compiler_params=PARAMS,
        cost_estimate=pl.CostEstimate(flops=0, bytes_accessed=n_dp * w.size, transcendentals=0),
    )(w)


def fetch(core, x_ref, g_ref, taken_ref, xs, gs, sems):
    tokens, model = x_ref.shape[1:]
    chunks = sems.shape[0]
    own, others = pl.ds(0, tokens), pl.ds(tokens, tokens)
    copies = []
    for j in range(chunks):
        cols = pl.ds(j * (model // chunks), model // chunks)
        copies.append([
            pltpu.make_async_copy(x_ref.at[core, :, cols], xs.at[own, cols], sems.at[j, 0]),
            pltpu.make_async_copy(taken_ref.at[0, :, cols], xs.at[others, cols], sems.at[j, 1]),
            pltpu.make_async_copy(g_ref.at[core, :, cols], gs.at[own, cols], sems.at[j, 2]),
            pltpu.make_async_copy(taken_ref.at[1, :, cols], gs.at[others, cols], sems.at[j, 3]),
        ])
        for copy in copies[-1]:
            copy.start()
    return copies


def adapter_kernel(
    count, core_ref, at_ref, x_ref, g_ref, taken_ref, w_ref, part_ref, up_ref, down_ref, up_send, down_send, edge_ref,
    xs, gs, ps, ms, loads, part_stores, stores, edge_sem
):
    is_down = core_ref[0] == 0
    slices, _, rank, width = w_ref.shape
    tokens, model = up_ref.shape
    chunks = loads.shape[0]
    per = slices // chunks
    own, others = pl.ds(0, tokens), pl.ds(tokens, tokens)
    fetches = fetch(core_ref[0], x_ref, g_ref, taken_ref, xs, gs, loads)

    u = jnp.zeros((2 * tokens, rank), F32)
    v = jnp.zeros((2 * tokens, rank), F32)
    squares = jnp.zeros((2 * tokens, 128), F32)
    for i in range(slices):
        if i % per == 0:
            for copy in fetches[i // per]:
                copy.wait()
        cols = pl.ds(i * width, width)
        x = xs[:, cols]
        u += lax.dot_general(x, w_ref[i, 0], ACROSS, preferred_element_type=F32)
        v += lax.dot_general(gs[:, cols], w_ref[i, 1], ACROSS, preferred_element_type=F32)
        xf = x.astype(F32)
        for j in range(width // 128):
            piece = xf[:, j * 128:(j + 1) * 128]
            squares += piece * piece
    scale = lax.rsqrt(jnp.sum(squares, axis=1, keepdims=True) / model + 1e-05)
    pre = scale * u
    sig = jax.nn.sigmoid(pre)
    hidden = (pre * sig).astype(jnp.bfloat16)
    dpre = v * (sig * (1.0 + pre * (1.0 - sig)))
    inner = jnp.sum(dpre * u, axis=1, keepdims=True) / model
    scaled = (scale * dpre).astype(jnp.bfloat16)
    back = inner * scale * scale * scale

    stored = []
    for i in range(slices):
        cols = pl.ds(i * width, width)
        ps[i, 0] = lax.dot_general(scaled, xs[:, cols], OVER_TOKENS, preferred_element_type=F32).astype(ps.dtype)
        ps[i, 1] = lax.dot_general(hidden, gs[:, cols], OVER_TOKENS, preferred_element_type=F32).astype(ps.dtype)
        xf, gf = xs[:, cols].astype(F32), gs[:, cols].astype(F32)
        y = (xf + jnp.dot(hidden, w_ref[i, 1], preferred_element_type=F32)).astype(ms.dtype)
        dx = (gf + jnp.dot(scaled, w_ref[i, 0], preferred_element_type=F32) - xf * back).astype(ms.dtype)
        ms[0, :, cols] = jnp.where(is_down, y, dx)
        ms[1, :, cols] = jnp.where(is_down, dx, y)
        if i % per == per - 1:
            j = i // per
            some = pl.ds(j * per, per)
            cols = pl.ds(j * (model // chunks), model // chunks)
            for copy in (
                pltpu.make_async_copy(ps.at[some], part_ref.at[some], part_stores.at[j]),
                pltpu.make_async_copy(ms.at[0, own, cols], up_ref.at[:, cols], stores.at[j, 0]),
                pltpu.make_async_copy(ms.at[1, own, cols], down_ref.at[:, cols], stores.at[j, 1]),
                pltpu.make_async_copy(ms.at[0, others, cols], up_send.at[:, cols], stores.at[j, 2]),
                pltpu.make_async_copy(ms.at[1, others, cols], down_send.at[:, cols], stores.at[j, 3]),
            ):
                copy.start()
                stored.append(copy)
    for way, position in ((0, count // 2 - 1), (1, count // 2)):
        @pl.when(at_ref[0] == position)
        def _():
            copy = pltpu.make_async_copy(ms.at[way, others], edge_ref, edge_sem)
            copy.start()
            copy.wait()
    for copy in stored:
        copy.wait()


def adapter(count, core, section, x, g, taken, w):
    tokens, model = x.shape[1:]
    one = pltpu.HBM((tokens, model), x.dtype)
    both = pltpu.VMEM((2 * tokens, model), x.dtype)
    return pl.pallas_call(
        functools.partial(adapter_kernel, count),
        out_shape=(pltpu.HBM(w.shape, w.dtype),) + (one,) * 5,
        in_specs=[SCALARS] * 2 + [ANYWHERE] * 3 + [WHOLE],
        out_specs=(ANYWHERE,) * 6,
        scratch_shapes=[
            both,
            both,
            pltpu.VMEM(w.shape, w.dtype),
            pltpu.VMEM((2, 2 * tokens, model), x.dtype),
            pltpu.SemaphoreType.DMA((4, 4)),
            pltpu.SemaphoreType.DMA((4,)),
            pltpu.SemaphoreType.DMA((4, 4)),
            pltpu.SemaphoreType.DMA,
        ],
        compiler_params=PARAMS,
        cost_estimate=pl.CostEstimate(flops=12 * tokens * w.size, bytes_accessed=12 << 20, transcendentals=0),
    )(core, section, x, g, taken, w)


def crossing_kernel(count, at_ref, up_ref, down_ref, out_ref, sem):
    for arrived, position in ((up_ref, count // 2), (down_ref, count // 2 - 1)):
        @pl.when(at_ref[0] == position)
        def _():
            copy = pltpu.make_async_copy(arrived, out_ref, sem)
            copy.start()
            copy.wait()


def crossing(count, section, up, down):
    return pl.pallas_call(
        functools.partial(crossing_kernel, count),
        out_shape=pltpu.HBM(up.shape, up.dtype),
        in_specs=[SCALARS] + [ANYWHERE] * 2,
        out_specs=ANYWHERE,
        scratch_shapes=[pltpu.SemaphoreType.DMA],
        compiler_params=PARAMS,
        cost_estimate=pl.CostEstimate(flops=0, bytes_accessed=4 * up.size, transcendentals=0),
    )(section, up, down)


def places(next_ref, prev_ref):
    return (
        (next_ref.at[0], prev_ref.at[1]),
        (prev_ref.at[0], next_ref.at[1]),
        (prev_ref.at[1], next_ref.at[0]),
        (next_ref.at[1], prev_ref.at[0]),
    )


def put(core, src, place, sem):
    for on, dst in enumerate(place):
        @pl.when(core == on)
        def _():
            pltpu.make_async_copy(src, dst, sem).start()


def assemble_kernel(core_ref, up_own, down_own, up_got, down_got, next_ref, prev_ref, stage, loads, sems):
    core = core_ref[0]
    where = places(next_ref, prev_ref)
    staging = [pltpu.make_async_copy(src, stage.at[i], loads.at[i]) for i, src in enumerate((up_got, down_got))]
    for copy in staging:
        copy.start()
    for i, src in enumerate((up_own, down_own)):
        put(core, src, where[i], sems.at[i])
    for i, copy in enumerate(staging):
        copy.wait()
        put(core, stage.at[i], where[2 + i], sems.at[2 + i])
    for i in range(4):
        pltpu.make_async_copy(stage.at[0], next_ref.at[0], sems.at[i]).wait()


def assemble(core, up_own, down_own, up_got, down_got):
    pair = pltpu.HBM((2,) + up_own.shape, up_own.dtype)
    return pl.pallas_call(
        assemble_kernel,
        out_shape=(pair, pair),
        in_specs=[SCALARS, WHOLE, WHOLE, ANYWHERE, ANYWHERE],
        out_specs=(ANYWHERE,) * 2,
        scratch_shapes=[
            pltpu.VMEM((2,) + up_own.shape, up_own.dtype),
            pltpu.SemaphoreType.DMA((2,)),
            pltpu.SemaphoreType.DMA((4,)),
        ],
        compiler_params=PARAMS,
        cost_estimate=pl.CostEstimate(flops=0, bytes_accessed=16 * up_own.size, transcendentals=0),
    )(core, up_own, down_own, in_hbm(up_got), in_hbm(down_got))


def amend_kernel(count, core_ref, at_ref, own_ref, got_ref, next_in, prev_in, next_ref, prev_ref, sems):
    core, section = core_ref[0], at_ref[0]
    where = places(next_ref, prev_ref)
    for way, position in ((0, count // 2), (1, count // 2 - 1)):
        @pl.when(section == position)
        def _():
            put(core, own_ref, where[way], sems.at[0])
            put(core, got_ref, where[2 + way], sems.at[1])
            pltpu.make_async_copy(own_ref, next_ref.at[0], sems.at[0]).wait()
            pltpu.make_async_copy(got_ref, next_ref.at[0], sems.at[1]).wait()


def amend(count, core, section, crossed_own, crossed_got, next_inputs, prev_grads):
    pair = pltpu.HBM(next_inputs.shape, next_inputs.dtype)
    return pl.pallas_call(
        functools.partial(amend_kernel, count),
        out_shape=(pair, pair),
        in_specs=[SCALARS] * 2 + [WHOLE] * 2 + [ANYWHERE] * 2,
        out_specs=(ANYWHERE,) * 2,
        scratch_shapes=[pltpu.SemaphoreType.DMA((2,))],
        input_output_aliases={4: 0, 5: 1},
        compiler_params=PARAMS,
        cost_estimate=pl.CostEstimate(flops=0, bytes_accessed=8 * crossed_own.size, transcendentals=0),
    )(core, section, crossed_own, crossed_got, in_hbm(next_inputs), in_hbm(prev_grads))


def add_kernel(sums_ref, partner_ref, out_ref):
    out_ref[0] = sums_ref[0] + partner_ref[1].astype(F32)
    out_ref[1] = sums_ref[1] + partner_ref[0].astype(F32)


def add_mirrored(sums, partner):
    return pl.pallas_call(
        add_kernel,
        out_shape=jax.ShapeDtypeStruct(sums.shape, F32),
        in_specs=[WHOLE] * 2,
        out_specs=WHOLE,
        compiler_params=PARAMS,
        cost_estimate=pl.CostEstimate(flops=4_000_000_000, bytes_accessed=2 << 20, transcendentals=0),
    )(sums, partner)


def moved(value, routes, n_dp):
    pairs = [(a * n_dp + d, b * n_dp + (d ^ turn)) for a, b, turn in routes for d in range(n_dp)]
    return lax.ppermute(value, ("section", "dp"), pairs)


def shards(section_inputs, out_grads, adapters):
    n_dp = lax.axis_size("dp")
    count = lax.axis_size("section")
    half = count // 2
    core = jnp.full((1,), lax.axis_index("dp") % 2, jnp.int32)
    section = jnp.full((1,), lax.axis_index("section"), jnp.int32)
    is_down = core[0] == 0
    swap = [(i, i ^ 1) for i in range(n_dp)]
    inputs, grads = section_inputs[:, 0], out_grads[:, 0]

    gathered = lax.all_to_all(spread(adapters[:, 0], n_dp), "dp", 0, 0, tiled=True)
    given = jnp.stack([jnp.where(is_down, inputs[1], inputs[0]), jnp.where(is_down, grads[1], grads[0])])
    taken = lax.ppermute(given, "dp", swap)
    x, g, taken = (in_hbm(a) for a in (inputs, grads, taken))
    parts, up_own, down_own, up_send, down_send, edge = adapter(count, core, section, x, g, taken, gathered)

    terms = lax.all_to_all(parts, "dp", 0, 0, tiled=True)
    sums = jnp.sum(terms.reshape((n_dp // 2, 2) + terms.shape[1:]).astype(F32), axis=0)

    group = n_dp // 2
    ups = [(i, i + 1) for i in range(count - 1) if i != half - 1]
    downs = [(i, i - 1) for i in range(1, count) if i != half]
    up_own = moved(up_own, [(a, b, 0) for a, b in ups] + [(half - 1, half, group)], n_dp)
    down_own = moved(down_own, [(a, b, 0) for a, b in downs] + [(half, half - 1, group)], n_dp)
    near = moved(edge, [(half - 1, 0, 1), (half, count - 1, 1)], n_dp)
    up_got = moved(up_send, [(a, b, 1) for a, b in ups], n_dp)
    down_got = moved(down_send, [(a, b, 1) for a, b in downs], n_dp)

    narrow = sums.astype(jnp.bfloat16)
    narrow, up_own, down_own, up_got, down_got = lax.optimization_barrier((narrow, up_own, down_own, up_got, down_got))
    partner = lax.ppermute(narrow, "section", [(i, count - 1 - i) for i in range(count)])
    crossed_own = moved(crossing(count, section, up_own, down_own), [(half, half, group), (half - 1, half - 1, group)], n_dp)
    crossed_got = moved(near, [(0, half, 0), (count - 1, half - 1, 0)], n_dp)
    next_inputs, prev_grads = assemble(core, up_own, down_own, up_got, down_got)
    partner, next_inputs, prev_grads = lax.optimization_barrier((partner, next_inputs, prev_grads))
    summed = add_mirrored(sums, partner)
    next_inputs, prev_grads = amend(count, core, section, crossed_own, crossed_got, next_inputs, prev_grads)
    return (next_inputs[:, None], prev_grads[:, None], summed[:, None])


def solution(mesh):
    in_specs = (
        P(None, "section", "dp", None),
        P(None, "section", "dp", None),
        P(None, "section", None, None, "dp"),
    )
    out_specs = (
        P(None, "section", "dp", None),
        P(None, "section", "dp", None),
        P(None, "section", None, None, "dp"),
    )
    return jax.shard_map(shards, mesh=mesh, in_specs=in_specs, out_specs=out_specs, check_vma=False)
```

```python
import functools

import jax
import jax.numpy as jnp
from jax import lax
from jax.experimental import pallas as pl
from jax.experimental.pallas import tpu as pltpu
from jax.sharding import PartitionSpec as P

WHOLE = pl.BlockSpec(memory_space=pltpu.VMEM)
ANYWHERE = pl.BlockSpec(memory_space=pl.ANY)
SCALARS = pl.BlockSpec(memory_space=pltpu.SMEM)
ACROSS = (((1,), (1,)), ((), ()))
OVER_TOKENS = (((0,), (0,)), ((), ()))
PARAMS = pltpu.CompilerParams(vmem_limit_bytes=12 << 20)
F32 = jnp.float32


def in_hbm(array):
    return pltpu.with_memory_space_constraint(array, pltpu.HBM)


def spread_kernel(w_ref, out_ref, sems):
    copies = [
        pltpu.make_async_copy(w_ref, out_ref.at[pl.ds(2 * i, 2)], sems.at[i]) for i in range(out_ref.shape[0] // 2)
    ]
    for copy in copies:
        copy.start()
    for copy in copies:
        copy.wait()


def spread(w, n_dp):
    return pl.pallas_call(
        spread_kernel,
        out_shape=pltpu.HBM((n_dp,) + w.shape[1:], w.dtype),
        in_specs=[WHOLE],
        out_specs=ANYWHERE,
        scratch_shapes=[pltpu.SemaphoreType.DMA((n_dp // 2,))],
        compiler_params=PARAMS,
        cost_estimate=pl.CostEstimate(flops=0, bytes_accessed=n_dp * w.size, transcendentals=0),
    )(w)


def fetch(core, x_ref, g_ref, taken_ref, xs, gs, sems):
    tokens, model = x_ref.shape[1:]
    chunks = sems.shape[0]
    own, others = pl.ds(0, tokens), pl.ds(tokens, tokens)
    copies = []
    for j in range(chunks):
        cols = pl.ds(j * (model // chunks), model // chunks)
        copies.append([
            pltpu.make_async_copy(x_ref.at[core, :, cols], xs.at[own, cols], sems.at[j, 0]),
            pltpu.make_async_copy(taken_ref.at[0, :, cols], xs.at[others, cols], sems.at[j, 1]),
            pltpu.make_async_copy(g_ref.at[core, :, cols], gs.at[own, cols], sems.at[j, 2]),
            pltpu.make_async_copy(taken_ref.at[1, :, cols], gs.at[others, cols], sems.at[j, 3]),
        ])
        for copy in copies[-1]:
            copy.start()
    return copies


def adapter_kernel(
    count, core_ref, at_ref, x_ref, g_ref, taken_ref, w_ref, part_ref, up_ref, down_ref, up_send, down_send, edge_ref,
    xs, gs, ps, ms, loads, part_stores, stores, edge_sem
):
    is_down = core_ref[0] == 0
    slices, _, rank, width = w_ref.shape
    tokens, model = up_ref.shape
    chunks = loads.shape[0]
    per = slices // chunks
    own, others = pl.ds(0, tokens), pl.ds(tokens, tokens)
    fetches = fetch(core_ref[0], x_ref, g_ref, taken_ref, xs, gs, loads)

    u = jnp.zeros((2 * tokens, rank), F32)
    v = jnp.zeros((2 * tokens, rank), F32)
    squares = jnp.zeros((2 * tokens, 128), F32)
    for i in range(slices):
        if i % per == 0:
            for copy in fetches[i // per]:
                copy.wait()
        cols = pl.ds(i * width, width)
        x = xs[:, cols]
        u += lax.dot_general(x, w_ref[i, 0], ACROSS, preferred_element_type=F32)
        v += lax.dot_general(gs[:, cols], w_ref[i, 1], ACROSS, preferred_element_type=F32)
        xf = x.astype(F32)
        for j in range(width // 128):
            piece = xf[:, j * 128:(j + 1) * 128]
            squares += piece * piece
    scale = lax.rsqrt(jnp.sum(squares, axis=1, keepdims=True) / model + 1e-05)
    pre = scale * u
    sig = jax.nn.sigmoid(pre)
    hidden = (pre * sig).astype(jnp.bfloat16)
    dpre = v * (sig * (1.0 + pre * (1.0 - sig)))
    inner = jnp.sum(dpre * u, axis=1, keepdims=True) / model
    scaled = (scale * dpre).astype(jnp.bfloat16)
    back = inner * scale * scale * scale

    stored = []
    for i in range(slices):
        cols = pl.ds(i * width, width)
        ps[i, 0] = lax.dot_general(scaled, xs[:, cols], OVER_TOKENS, preferred_element_type=F32).astype(ps.dtype)
        ps[i, 1] = lax.dot_general(hidden, gs[:, cols], OVER_TOKENS, preferred_element_type=F32).astype(ps.dtype)
        xf, gf = xs[:, cols].astype(F32), gs[:, cols].astype(F32)
        y = (xf + jnp.dot(hidden, w_ref[i, 1], preferred_element_type=F32)).astype(ms.dtype)
        dx = (gf + jnp.dot(scaled, w_ref[i, 0], preferred_element_type=F32) - xf * back).astype(ms.dtype)
        ms[0, :, cols] = jnp.where(is_down, y, dx)
        ms[1, :, cols] = jnp.where(is_down, dx, y)
        if i % per == per - 1:
            j = i // per
            some = pl.ds(j * per, per)
            cols = pl.ds(j * (model // chunks), model // chunks)
            for copy in (
                pltpu.make_async_copy(ps.at[some], part_ref.at[some], part_stores.at[j]),
                pltpu.make_async_copy(ms.at[0, own, cols], up_ref.at[:, cols], stores.at[j, 0]),
                pltpu.make_async_copy(ms.at[1, own, cols], down_ref.at[:, cols], stores.at[j, 1]),
                pltpu.make_async_copy(ms.at[0, others, cols], up_send.at[:, cols], stores.at[j, 2]),
                pltpu.make_async_copy(ms.at[1, others, cols], down_send.at[:, cols], stores.at[j, 3]),
            ):
                copy.start()
                stored.append(copy)
    for way, position in ((0, count // 2 - 1), (1, count // 2)):
        @pl.when(at_ref[0] == position)
        def _():
            copy = pltpu.make_async_copy(ms.at[way, others], edge_ref, edge_sem)
            copy.start()
            copy.wait()
    for copy in stored:
        copy.wait()


def adapter(count, core, section, x, g, taken, w):
    tokens, model = x.shape[1:]
    one = pltpu.HBM((tokens, model), x.dtype)
    both = pltpu.VMEM((2 * tokens, model), x.dtype)
    return pl.pallas_call(
        functools.partial(adapter_kernel, count),
        out_shape=(pltpu.HBM(w.shape, w.dtype),) + (one,) * 5,
        in_specs=[SCALARS] * 2 + [ANYWHERE] * 3 + [WHOLE],
        out_specs=(ANYWHERE,) * 6,
        scratch_shapes=[
            both,
            both,
            pltpu.VMEM(w.shape, w.dtype),
            pltpu.VMEM((2, 2 * tokens, model), x.dtype),
            pltpu.SemaphoreType.DMA((4, 4)),
            pltpu.SemaphoreType.DMA((4,)),
            pltpu.SemaphoreType.DMA((4, 4)),
            pltpu.SemaphoreType.DMA,
        ],
        compiler_params=PARAMS,
        cost_estimate=pl.CostEstimate(flops=12 * tokens * w.size, bytes_accessed=12 << 20, transcendentals=0),
    )(core, section, x, g, taken, w)


def crossing_kernel(count, at_ref, up_ref, down_ref, out_ref, sem):
    for arrived, position in ((up_ref, count // 2), (down_ref, count // 2 - 1)):
        @pl.when(at_ref[0] == position)
        def _():
            copy = pltpu.make_async_copy(arrived, out_ref, sem)
            copy.start()
            copy.wait()


def crossing(count, section, up, down):
    return pl.pallas_call(
        functools.partial(crossing_kernel, count),
        out_shape=pltpu.HBM(up.shape, up.dtype),
        in_specs=[SCALARS] + [ANYWHERE] * 2,
        out_specs=ANYWHERE,
        scratch_shapes=[pltpu.SemaphoreType.DMA],
        compiler_params=PARAMS,
        cost_estimate=pl.CostEstimate(flops=0, bytes_accessed=4 * up.size, transcendentals=0),
    )(section, up, down)


def places(next_ref, prev_ref):
    return (
        (next_ref.at[0], prev_ref.at[1]),
        (prev_ref.at[0], next_ref.at[1]),
        (prev_ref.at[1], next_ref.at[0]),
        (next_ref.at[1], prev_ref.at[0]),
    )


def put(core, src, place, sem):
    for on, dst in enumerate(place):
        @pl.when(core == on)
        def _():
            pltpu.make_async_copy(src, dst, sem).start()


def assemble_kernel(core_ref, up_own, down_own, up_got, down_got, next_ref, prev_ref, stage, loads, sems):
    core = core_ref[0]
    where = places(next_ref, prev_ref)
    staging = [pltpu.make_async_copy(src, stage.at[i], loads.at[i]) for i, src in enumerate((up_got, down_got))]
    for copy in staging:
        copy.start()
    for i, src in enumerate((up_own, down_own)):
        put(core, src, where[i], sems.at[i])
    for i, copy in enumerate(staging):
        copy.wait()
        put(core, stage.at[i], where[2 + i], sems.at[2 + i])
    for i in range(4):
        pltpu.make_async_copy(stage.at[0], next_ref.at[0], sems.at[i]).wait()


def assemble(core, up_own, down_own, up_got, down_got):
    pair = pltpu.HBM((2,) + up_own.shape, up_own.dtype)
    return pl.pallas_call(
        assemble_kernel,
        out_shape=(pair, pair),
        in_specs=[SCALARS, WHOLE, WHOLE, ANYWHERE, ANYWHERE],
        out_specs=(ANYWHERE,) * 2,
        scratch_shapes=[
            pltpu.VMEM((2,) + up_own.shape, up_own.dtype),
            pltpu.SemaphoreType.DMA((2,)),
            pltpu.SemaphoreType.DMA((4,)),
        ],
        compiler_params=PARAMS,
        cost_estimate=pl.CostEstimate(flops=0, bytes_accessed=16 * up_own.size, transcendentals=0),
    )(core, up_own, down_own, in_hbm(up_got), in_hbm(down_got))


def amend_kernel(count, core_ref, at_ref, own_ref, got_ref, next_in, prev_in, next_ref, prev_ref, sems):
    core, section = core_ref[0], at_ref[0]
    where = places(next_ref, prev_ref)
    for way, position in ((0, count // 2), (1, count // 2 - 1)):
        @pl.when(section == position)
        def _():
            put(core, own_ref, where[way], sems.at[0])
            put(core, got_ref, where[2 + way], sems.at[1])
            pltpu.make_async_copy(own_ref, next_ref.at[0], sems.at[0]).wait()
            pltpu.make_async_copy(got_ref, next_ref.at[0], sems.at[1]).wait()


def amend(count, core, section, crossed_own, crossed_got, next_inputs, prev_grads):
    pair = pltpu.HBM(next_inputs.shape, next_inputs.dtype)
    return pl.pallas_call(
        functools.partial(amend_kernel, count),
        out_shape=(pair, pair),
        in_specs=[SCALARS] * 2 + [WHOLE] * 2 + [ANYWHERE] * 2,
        out_specs=(ANYWHERE,) * 2,
        scratch_shapes=[pltpu.SemaphoreType.DMA((2,))],
        input_output_aliases={4: 0, 5: 1},
        compiler_params=PARAMS,
        cost_estimate=pl.CostEstimate(flops=0, bytes_accessed=8 * crossed_own.size, transcendentals=0),
    )(core, section, crossed_own, crossed_got, in_hbm(next_inputs), in_hbm(prev_grads))


def add_kernel(sums_ref, partner_ref, out_ref):
    out_ref[0] = sums_ref[0] + partner_ref[1].astype(F32)
    out_ref[1] = sums_ref[1] + partner_ref[0].astype(F32)


def add_mirrored(sums, partner):
    return pl.pallas_call(
        add_kernel,
        out_shape=jax.ShapeDtypeStruct(sums.shape, F32),
        in_specs=[WHOLE] * 2,
        out_specs=WHOLE,
        compiler_params=PARAMS,
        cost_estimate=pl.CostEstimate(flops=4_000_000_000, bytes_accessed=2 << 20, transcendentals=0),
    )(sums, partner)


def moved(value, routes, n_dp):
    pairs = [(a * n_dp + d, b * n_dp + (d ^ turn)) for a, b, turn in routes for d in range(n_dp)]
    return lax.ppermute(value, ("section", "dp"), pairs)


def shards(section_inputs, out_grads, adapters):
    n_dp = lax.axis_size("dp")
    count = lax.axis_size("section")
    half = count // 2
    core = jnp.full((1,), lax.axis_index("dp") % 2, jnp.int32)
    section = jnp.full((1,), lax.axis_index("section"), jnp.int32)
    is_down = core[0] == 0
    swap = [(i, i ^ 1) for i in range(n_dp)]
    inputs, grads = section_inputs[:, 0], out_grads[:, 0]

    gathered = lax.all_to_all(spread(adapters[:, 0], n_dp), "dp", 0, 0, tiled=True)
    given = jnp.stack([jnp.where(is_down, inputs[1], inputs[0]), jnp.where(is_down, grads[1], grads[0])])
    taken = lax.ppermute(given, "dp", swap)
    x, g, taken = (in_hbm(a) for a in (inputs, grads, taken))
    parts, up_own, down_own, up_send, down_send, edge = adapter(count, core, section, x, g, taken, gathered)

    terms = lax.all_to_all(parts, "dp", 0, 0, tiled=True)
    sums = jnp.sum(terms.reshape((n_dp // 2, 2) + terms.shape[1:]).astype(F32), axis=0)

    group = n_dp // 2
    ups = [(i, i + 1) for i in range(count - 1) if i != half - 1]
    downs = [(i, i - 1) for i in range(1, count) if i != half]
    up_own = moved(up_own, [(a, b, 0) for a, b in ups] + [(half - 1, half, group)], n_dp)
    down_own = moved(down_own, [(a, b, 0) for a, b in downs] + [(half, half - 1, group)], n_dp)
    near = moved(edge, [(half - 1, 0, 1), (half, count - 1, 1)], n_dp)
    up_got = moved(up_send, [(a, b, 1) for a, b in ups], n_dp)
    down_got = moved(down_send, [(a, b, 1) for a, b in downs], n_dp)

    narrow = sums.astype(jnp.bfloat16)
    narrow, up_own, down_own = lax.optimization_barrier((narrow, up_own, down_own))
    partner = lax.ppermute(narrow, "section", [(i, count - 1 - i) for i in range(count)])
    near, up_got, down_got = lax.optimization_barrier((near, up_got, down_got))
    crossed_own = moved(crossing(count, section, up_own, down_own), [(half, half, group), (half - 1, half - 1, group)], n_dp)
    crossed_got = moved(near, [(0, half, 0), (count - 1, half - 1, 0)], n_dp)
    next_inputs, prev_grads = assemble(core, up_own, down_own, up_got, down_got)
    partner, next_inputs, prev_grads = lax.optimization_barrier((partner, next_inputs, prev_grads))
    summed = add_mirrored(sums, partner)
    next_inputs, prev_grads = amend(count, core, section, crossed_own, crossed_got, next_inputs, prev_grads)
    return (next_inputs[:, None], prev_grads[:, None], summed[:, None])


def solution(mesh):
    in_specs = (
        P(None, "section", "dp", None),
        P(None, "section", "dp", None),
        P(None, "section", None, None, "dp"),
    )
    out_specs = (
        P(None, "section", "dp", None),
        P(None, "section", "dp", None),
        P(None, "section", None, None, "dp"),
    )
    return jax.shard_map(shards, mesh=mesh, in_specs=in_specs, out_specs=out_specs, check_vma=False)
```

```python
import functools

import jax
import jax.numpy as jnp
from jax import lax
from jax.experimental import pallas as pl
from jax.experimental.pallas import tpu as pltpu
from jax.sharding import PartitionSpec as P

WHOLE = pl.BlockSpec(memory_space=pltpu.VMEM)
ANYWHERE = pl.BlockSpec(memory_space=pl.ANY)
SCALARS = pl.BlockSpec(memory_space=pltpu.SMEM)
ACROSS = (((1,), (1,)), ((), ()))
OVER_TOKENS = (((0,), (0,)), ((), ()))
PARAMS = pltpu.CompilerParams(vmem_limit_bytes=12 << 20)
F32 = jnp.float32


def in_hbm(array):
    return pltpu.with_memory_space_constraint(array, pltpu.HBM)


def spread_kernel(w_ref, out_ref, sems):
    copies = [
        pltpu.make_async_copy(w_ref, out_ref.at[pl.ds(2 * i, 2)], sems.at[i]) for i in range(out_ref.shape[0] // 2)
    ]
    for copy in copies:
        copy.start()
    for copy in copies:
        copy.wait()


def spread(w, n_dp):
    return pl.pallas_call(
        spread_kernel,
        out_shape=pltpu.HBM((n_dp,) + w.shape[1:], w.dtype),
        in_specs=[WHOLE],
        out_specs=ANYWHERE,
        scratch_shapes=[pltpu.SemaphoreType.DMA((n_dp // 2,))],
        compiler_params=PARAMS,
        cost_estimate=pl.CostEstimate(flops=0, bytes_accessed=n_dp * w.size, transcendentals=0),
    )(w)


def fetch(core, x_ref, g_ref, taken_ref, xs, gs, sems):
    tokens, model = x_ref.shape[1:]
    chunks = sems.shape[0]
    own, others = pl.ds(0, tokens), pl.ds(tokens, tokens)
    copies = []
    for j in range(chunks):
        cols = pl.ds(j * (model // chunks), model // chunks)
        copies.append([
            pltpu.make_async_copy(x_ref.at[core, :, cols], xs.at[own, cols], sems.at[j, 0]),
            pltpu.make_async_copy(taken_ref.at[0, :, cols], xs.at[others, cols], sems.at[j, 1]),
            pltpu.make_async_copy(g_ref.at[core, :, cols], gs.at[own, cols], sems.at[j, 2]),
            pltpu.make_async_copy(taken_ref.at[1, :, cols], gs.at[others, cols], sems.at[j, 3]),
        ])
        for copy in copies[-1]:
            copy.start()
    return copies


def adapter_kernel(
    count, core_ref, at_ref, x_ref, g_ref, taken_ref, w_ref, part_ref, up_ref, down_ref, up_send, down_send, edge_ref,
    xs, gs, ps, ms, loads, part_stores, stores, edge_sems
):
    is_down = core_ref[0] == 0
    slices, _, rank, width = w_ref.shape
    tokens, model = up_ref.shape
    chunks = loads.shape[0]
    per = slices // chunks
    own, others = pl.ds(0, tokens), pl.ds(tokens, tokens)
    fetches = fetch(core_ref[0], x_ref, g_ref, taken_ref, xs, gs, loads)

    u = jnp.zeros((2 * tokens, rank), F32)
    v = jnp.zeros((2 * tokens, rank), F32)
    squares = jnp.zeros((2 * tokens, 128), F32)
    for i in range(slices):
        if i % per == 0:
            for copy in fetches[i // per]:
                copy.wait()
        cols = pl.ds(i * width, width)
        x = xs[:, cols]
        u += lax.dot_general(x, w_ref[i, 0], ACROSS, preferred_element_type=F32)
        v += lax.dot_general(gs[:, cols], w_ref[i, 1], ACROSS, preferred_element_type=F32)
        xf = x.astype(F32)
        for j in range(width // 128):
            piece = xf[:, j * 128:(j + 1) * 128]
            squares += piece * piece
    scale = lax.rsqrt(jnp.sum(squares, axis=1, keepdims=True) / model + 1e-05)
    pre = scale * u
    sig = jax.nn.sigmoid(pre)
    hidden = (pre * sig).astype(jnp.bfloat16)
    dpre = v * (sig * (1.0 + pre * (1.0 - sig)))
    inner = jnp.sum(dpre * u, axis=1, keepdims=True) / model
    scaled = (scale * dpre).astype(jnp.bfloat16)
    back = inner * scale * scale * scale

    stored = []
    for i in range(slices):
        cols = pl.ds(i * width, width)
        ps[i, 0] = lax.dot_general(scaled, xs[:, cols], OVER_TOKENS, preferred_element_type=F32).astype(ps.dtype)
        ps[i, 1] = lax.dot_general(hidden, gs[:, cols], OVER_TOKENS, preferred_element_type=F32).astype(ps.dtype)
        xf, gf = xs[:, cols].astype(F32), gs[:, cols].astype(F32)
        y = (xf + jnp.dot(hidden, w_ref[i, 1], preferred_element_type=F32)).astype(ms.dtype)
        dx = (gf + jnp.dot(scaled, w_ref[i, 0], preferred_element_type=F32) - xf * back).astype(ms.dtype)
        ms[0, :, cols] = jnp.where(is_down, y, dx)
        ms[1, :, cols] = jnp.where(is_down, dx, y)
        if i % per == per - 1:
            j = i // per
            some = pl.ds(j * per, per)
            cols = pl.ds(j * (model // chunks), model // chunks)
            for copy in (
                pltpu.make_async_copy(ps.at[some], part_ref.at[some], part_stores.at[j]),
                pltpu.make_async_copy(ms.at[0, own, cols], up_ref.at[:, cols], stores.at[j, 0]),
                pltpu.make_async_copy(ms.at[1, own, cols], down_ref.at[:, cols], stores.at[j, 1]),
                pltpu.make_async_copy(ms.at[0, others, cols], up_send.at[:, cols], stores.at[j, 2]),
                pltpu.make_async_copy(ms.at[1, others, cols], down_send.at[:, cols], stores.at[j, 3]),
            ):
                copy.start()
                stored.append(copy)
            for way, position in ((0, count // 2 - 1), (1, count // 2)):
                @pl.when(at_ref[0] == position)
                def _():
                    pltpu.make_async_copy(ms.at[way, others, cols], edge_ref.at[:, cols], edge_sems.at[j]).start()
    for copy in stored:
        copy.wait()
    for position in (count // 2 - 1, count // 2):
        @pl.when(at_ref[0] == position)
        def _():
            for j in range(chunks):
                cols = pl.ds(j * (model // chunks), model // chunks)
                pltpu.make_async_copy(ms.at[0, others, cols], edge_ref.at[:, cols], edge_sems.at[j]).wait()


def adapter(count, core, section, x, g, taken, w):
    tokens, model = x.shape[1:]
    one = pltpu.HBM((tokens, model), x.dtype)
    both = pltpu.VMEM((2 * tokens, model), x.dtype)
    return pl.pallas_call(
        functools.partial(adapter_kernel, count),
        out_shape=(pltpu.HBM(w.shape, w.dtype),) + (one,) * 5,
        in_specs=[SCALARS] * 2 + [ANYWHERE] * 3 + [WHOLE],
        out_specs=(ANYWHERE,) * 6,
        scratch_shapes=[
            both,
            both,
            pltpu.VMEM(w.shape, w.dtype),
            pltpu.VMEM((2, 2 * tokens, model), x.dtype),
            pltpu.SemaphoreType.DMA((4, 4)),
            pltpu.SemaphoreType.DMA((4,)),
            pltpu.SemaphoreType.DMA((4, 4)),
            pltpu.SemaphoreType.DMA((4,)),
        ],
        compiler_params=PARAMS,
        cost_estimate=pl.CostEstimate(flops=12 * tokens * w.size, bytes_accessed=12 << 20, transcendentals=0),
    )(core, section, x, g, taken, w)


def crossing_kernel(count, at_ref, up_ref, down_ref, out_ref, sem):
    for arrived, position in ((up_ref, count // 2), (down_ref, count // 2 - 1)):
        @pl.when(at_ref[0] == position)
        def _():
            copy = pltpu.make_async_copy(arrived, out_ref, sem)
            copy.start()
            copy.wait()


def crossing(count, section, up, down):
    return pl.pallas_call(
        functools.partial(crossing_kernel, count),
        out_shape=pltpu.HBM(up.shape, up.dtype),
        in_specs=[SCALARS] + [ANYWHERE] * 2,
        out_specs=ANYWHERE,
        scratch_shapes=[pltpu.SemaphoreType.DMA],
        compiler_params=PARAMS,
        cost_estimate=pl.CostEstimate(flops=0, bytes_accessed=4 * up.size, transcendentals=0),
    )(section, up, down)


def places(next_ref, prev_ref):
    return (
        (next_ref.at[0], prev_ref.at[1]),
        (prev_ref.at[0], next_ref.at[1]),
        (prev_ref.at[1], next_ref.at[0]),
        (next_ref.at[1], prev_ref.at[0]),
    )


def put(core, src, place, sem):
    for on, dst in enumerate(place):
        @pl.when(core == on)
        def _():
            pltpu.make_async_copy(src, dst, sem).start()


def assemble_kernel(core_ref, up_own, down_own, up_got, down_got, next_ref, prev_ref, stage, loads, sems):
    core = core_ref[0]
    where = places(next_ref, prev_ref)
    staging = [pltpu.make_async_copy(src, stage.at[i], loads.at[i]) for i, src in enumerate((up_got, down_got))]
    for copy in staging:
        copy.start()
    for i, src in enumerate((up_own, down_own)):
        put(core, src, where[i], sems.at[i])
    for i, copy in enumerate(staging):
        copy.wait()
        put(core, stage.at[i], where[2 + i], sems.at[2 + i])
    for i in range(4):
        pltpu.make_async_copy(stage.at[0], next_ref.at[0], sems.at[i]).wait()


def assemble(core, up_own, down_own, up_got, down_got):
    pair = pltpu.HBM((2,) + up_own.shape, up_own.dtype)
    return pl.pallas_call(
        assemble_kernel,
        out_shape=(pair, pair),
        in_specs=[SCALARS, WHOLE, WHOLE, ANYWHERE, ANYWHERE],
        out_specs=(ANYWHERE,) * 2,
        scratch_shapes=[
            pltpu.VMEM((2,) + up_own.shape, up_own.dtype),
            pltpu.SemaphoreType.DMA((2,)),
            pltpu.SemaphoreType.DMA((4,)),
        ],
        compiler_params=PARAMS,
        cost_estimate=pl.CostEstimate(flops=0, bytes_accessed=16 * up_own.size, transcendentals=0),
    )(core, up_own, down_own, in_hbm(up_got), in_hbm(down_got))


def amend_kernel(count, core_ref, at_ref, own_ref, got_ref, next_in, prev_in, next_ref, prev_ref, sems):
    core, section = core_ref[0], at_ref[0]
    where = places(next_ref, prev_ref)
    for way, position in ((0, count // 2), (1, count // 2 - 1)):
        @pl.when(section == position)
        def _():
            put(core, own_ref, where[way], sems.at[0])
            put(core, got_ref, where[2 + way], sems.at[1])
            pltpu.make_async_copy(own_ref, next_ref.at[0], sems.at[0]).wait()
            pltpu.make_async_copy(got_ref, next_ref.at[0], sems.at[1]).wait()


def amend(count, core, section, crossed_own, crossed_got, next_inputs, prev_grads):
    pair = pltpu.HBM(next_inputs.shape, next_inputs.dtype)
    return pl.pallas_call(
        functools.partial(amend_kernel, count),
        out_shape=(pair, pair),
        in_specs=[SCALARS] * 2 + [WHOLE] * 2 + [ANYWHERE] * 2,
        out_specs=(ANYWHERE,) * 2,
        scratch_shapes=[pltpu.SemaphoreType.DMA((2,))],
        input_output_aliases={4: 0, 5: 1},
        compiler_params=PARAMS,
        cost_estimate=pl.CostEstimate(flops=0, bytes_accessed=8 * crossed_own.size, transcendentals=0),
    )(core, section, crossed_own, crossed_got, in_hbm(next_inputs), in_hbm(prev_grads))


def add_kernel(sums_ref, partner_ref, out_ref):
    out_ref[0] = sums_ref[0] + partner_ref[1].astype(F32)
    out_ref[1] = sums_ref[1] + partner_ref[0].astype(F32)


def add_mirrored(sums, partner):
    return pl.pallas_call(
        add_kernel,
        out_shape=jax.ShapeDtypeStruct(sums.shape, F32),
        in_specs=[WHOLE] * 2,
        out_specs=WHOLE,
        compiler_params=PARAMS,
        cost_estimate=pl.CostEstimate(flops=4_000_000_000, bytes_accessed=2 << 20, transcendentals=0),
    )(sums, partner)


def moved(value, routes, n_dp):
    pairs = [(a * n_dp + d, b * n_dp + (d ^ turn)) for a, b, turn in routes for d in range(n_dp)]
    return lax.ppermute(value, ("section", "dp"), pairs)


def shards(section_inputs, out_grads, adapters):
    n_dp = lax.axis_size("dp")
    count = lax.axis_size("section")
    half = count // 2
    core = jnp.full((1,), lax.axis_index("dp") % 2, jnp.int32)
    section = jnp.full((1,), lax.axis_index("section"), jnp.int32)
    is_down = core[0] == 0
    swap = [(i, i ^ 1) for i in range(n_dp)]
    inputs, grads = section_inputs[:, 0], out_grads[:, 0]

    gathered = lax.all_to_all(spread(adapters[:, 0], n_dp), "dp", 0, 0, tiled=True)
    given = jnp.stack([jnp.where(is_down, inputs[1], inputs[0]), jnp.where(is_down, grads[1], grads[0])])
    taken = lax.ppermute(given, "dp", swap)
    x, g, taken = (in_hbm(a) for a in (inputs, grads, taken))
    parts, up_own, down_own, up_send, down_send, edge = adapter(count, core, section, x, g, taken, gathered)

    terms = lax.all_to_all(parts, "dp", 0, 0, tiled=True)
    sums = jnp.sum(terms.reshape((n_dp // 2, 2) + terms.shape[1:]).astype(F32), axis=0)

    group = n_dp // 2
    ups = [(i, i + 1) for i in range(count - 1) if i != half - 1]
    downs = [(i, i - 1) for i in range(1, count) if i != half]
    up_own = moved(up_own, [(a, b, 0) for a, b in ups] + [(half - 1, half, group)], n_dp)
    down_own = moved(down_own, [(a, b, 0) for a, b in downs] + [(half, half - 1, group)], n_dp)
    near = moved(edge, [(half - 1, 0, 1), (half, count - 1, 1)], n_dp)
    up_got = moved(up_send, [(a, b, 1) for a, b in ups], n_dp)
    down_got = moved(down_send, [(a, b, 1) for a, b in downs], n_dp)

    narrow = sums.astype(jnp.bfloat16)
    narrow, up_own, down_own = lax.optimization_barrier((narrow, up_own, down_own))
    partner = lax.ppermute(narrow, "section", [(i, count - 1 - i) for i in range(count)])
    near, up_got, down_got = lax.optimization_barrier((near, up_got, down_got))
    crossed_own = moved(crossing(count, section, up_own, down_own), [(half, half, group), (half - 1, half - 1, group)], n_dp)
    crossed_got = moved(near, [(0, half, 0), (count - 1, half - 1, 0)], n_dp)
    next_inputs, prev_grads = assemble(core, up_own, down_own, up_got, down_got)
    partner, next_inputs, prev_grads = lax.optimization_barrier((partner, next_inputs, prev_grads))
    summed = add_mirrored(sums, partner)
    next_inputs, prev_grads = amend(count, core, section, crossed_own, crossed_got, next_inputs, prev_grads)
    return (next_inputs[:, None], prev_grads[:, None], summed[:, None])


def solution(mesh):
    in_specs = (
        P(None, "section", "dp", None),
        P(None, "section", "dp", None),
        P(None, "section", None, None, "dp"),
    )
    out_specs = (
        P(None, "section", "dp", None),
        P(None, "section", "dp", None),
        P(None, "section", None, None, "dp"),
    )
    return jax.shard_map(shards, mesh=mesh, in_specs=in_specs, out_specs=out_specs, check_vma=False)
```
